128 devices in a mesh: row: 16 (over x, z_lo, core), col: 8 (over y, z_hi).
Axes of the slice: x: 4, y: 4, z: 4 (z_hi: 2, z_lo: 2; z = z_hi * 2 + z_lo), core: 2. Of those that a mesh axis runs over, the one named last changes fastest.
Arguments:
- pair: bfloat16 [512, 512, 128], P('row', 'col'), may hold values from -6 to 6
- pad_mask: int32 [512], replicated, may hold values 0 or 1
- valid_flags: int32 [512], replicated, may hold values 0 or 1
- w_in: bfloat16 [2, 128, 512], replicated, may hold values from -0.5 to 0.5
- w_gate: bfloat16 [2, 128, 128], replicated, may hold values from -0.5 to 0.5
- w_out: bfloat16 [2, 128, 128], replicated, may hold values from -0.5 to 0.5
- gains: float32 [2, 2, 128], replicated, may hold values from 0.1 to 1.9
- shifts: float32 [2, 2, 128], replicated, may hold values from -3 to 3
Outputs:
- result: bfloat16 [512, 512, 128], P('row', 'col')
The draws below stay inside these ranges and needn't reach their ends.
All inputs are finite; a program needn't handle non-finite values.
Results may differ from the reference program's by a relative error of at most 0.013.
Values may be sent and summed in bfloat16 or wider, within the bound.
A program may use at most 128 MiB of HBM per device.

```python
import jax
import jax.numpy as jnp
from jax import lax

C = 128
H = 128
N = 512


def set_ends(result, own_key, low, largest):
    extent = result.shape
    index_at = [jax.random.randint(jax.random.fold_in(own_key, axis), (), 0, extent[axis]) for axis in range(len(extent))]
    result = result.at[tuple(index_at)].set(low)
    longest = extent.index(max(extent))
    index_at[longest] = (index_at[longest] + 1) % extent[longest]
    return result.at[tuple(index_at)].set(largest)


def levels(own_key, dims, split, low, largest):
    def one(dim, parts):
        heights = jax.random.uniform(jax.random.fold_in(jax.random.fold_in(own_key, 6), dim), (parts,), jnp.float32, low / len(split), largest / len(split))
        return jnp.repeat(jnp.exp(heights), dims[dim] // parts).reshape((-1,) + (1,) * (len(dims) - dim - 1))

    level = one(*split[0])
    for cut in split[1:]:
        level = level * one(*cut)
    return level


def noise(rng, shape, width, most, pieces=(), held_as=jnp.bfloat16):
    factor_of = levels(rng, shape, pieces, -0.22, 0.18) if pieces else 1.0
    result = jax.random.normal(rng, shape, jnp.float32) * width * factor_of
    return jnp.minimum(jnp.maximum(result, -most), most).astype(held_as)


def setup_inputs(seed: int = 0) -> dict:
    key_of = jax.random.split(jax.random.key(seed), 9)
    pair = noise(key_of[0], (N, N, C), 1.0, 6.0, ((0, 16), (1, 8)))
    pad_mask = set_ends((jax.random.randint(key_of[1], (N,), 0, 8) < 7).astype(jnp.int32), jax.random.fold_in(key_of[1], 1), 0, 1)
    valid_flags = set_ends((jax.random.randint(key_of[2], (N,), 0, 4) < 3).astype(jnp.int32), jax.random.fold_in(key_of[2], 1), 0, 1)
    w_in = noise(key_of[3], (2, C, 4 * H), C ** -0.5, 0.5)
    w_gate = noise(key_of[4], (2, C, C), C ** -0.5, 0.5)
    w_out = noise(key_of[5], (2, H, C), H ** -0.5, 0.5)
    gains = jnp.clip(1.0 + 0.18 * jax.random.normal(key_of[6], (2, 2, C), jnp.float32), 0.1, 1.9)
    shifts = noise(key_of[7], (2, 2, C), 0.5, 3.0, (), jnp.float32)
    return {"pair": pair, "pad_mask": pad_mask, "valid_flags": valid_flags, "w_in": w_in, "w_gate": w_gate, "w_out": w_out, "gains": gains, "shifts": shifts}


EPS = 1e-05

def layer_norm(values, gain, shift):
    center = lax.optimization_barrier(jnp.mean(values, axis=-1, keepdims=True))
    centred = values - center
    variance = lax.optimization_barrier(jnp.mean(centred * centred, axis=-1, keepdims=True))
    return centred * lax.rsqrt(variance + EPS) * gain + shift

def project_pair(pair, pad_rows, pad_cols, weight_in, weight_gate, gain_pair, shift_pair):
    normed = layer_norm(pair.astype(jnp.float32), gain_pair[0], shift_pair[0]).astype(jnp.bfloat16)
    hidden = weight_in.shape[1] // 4
    flat = normed.reshape(-1, normed.shape[-1])
    projected = jnp.dot(flat, weight_in, preferred_element_type=jnp.float32)
    projected = projected.reshape(normed.shape[0], normed.shape[1], 4 * hidden)
    pair_mask = (pad_rows.astype(jnp.float32)[:, None] * pad_cols.astype(jnp.float32)[None, :])[..., None]
    left_side = (jax.nn.sigmoid(projected[..., 2 * hidden:3 * hidden]) * projected[..., :hidden] * pair_mask).astype(jnp.bfloat16)
    right_side = (jax.nn.sigmoid(projected[..., 3 * hidden:]) * projected[..., hidden:2 * hidden] * pair_mask).astype(jnp.bfloat16)
    gating = jax.nn.sigmoid(jnp.dot(flat, weight_gate, preferred_element_type=jnp.float32)).reshape(pair.shape)
    return (left_side, right_side, gating)

def finish_pair(pair, mixed, gating, valid_rows, valid_cols, weight_out, gain_pair, shift_pair):
    normed = layer_norm(mixed, gain_pair[1], shift_pair[1]).astype(jnp.bfloat16)
    flat = normed.reshape(-1, normed.shape[-1])
    update = jnp.dot(flat, weight_out, preferred_element_type=jnp.float32).reshape(pair.shape)
    weight = (valid_rows.astype(jnp.float32)[:, None] * valid_cols.astype(jnp.float32)[None, :])[..., None]
    return (pair.astype(jnp.float32) + gating * update * weight).astype(jnp.bfloat16)

def reference(pair, pad_mask, valid_flags, w_in, w_gate, w_out, gains, shifts):
    left_side, right_side, gating = project_pair(pair, pad_mask, pad_mask, w_in[0], w_gate[0], gains[0], shifts[0])
    mixed = jnp.einsum('ikh,jkh->ijh', left_side.astype(jnp.float32), right_side.astype(jnp.float32))
    first = finish_pair(pair, mixed, gating, valid_flags, valid_flags, w_out[0], gains[0], shifts[0])
    left_side, right_side, gating = project_pair(first, pad_mask, pad_mask, w_in[1], w_gate[1], gains[1], shifts[1])
    mixed = jnp.einsum('kih,kjh->ijh', left_side.astype(jnp.float32), right_side.astype(jnp.float32))
    return finish_pair(first, mixed, gating, valid_flags, valid_flags, w_out[1], gains[1], shifts[1])
```

```python
import functools

import jax
import jax.numpy as jnp
from jax import lax
from jax.experimental import pallas as pl
from jax.experimental.pallas import tpu as pltpu
from jax.sharding import PartitionSpec as P

EPS = 1e-05
MESH = pl.DeviceIdType.MESH
F32 = jnp.float32
BF16 = jnp.bfloat16
T = 16
HALF = 64


def sigmoid(v):
    return jax.nn.sigmoid(v)


def kernel(
    nr, nc, pair_ref, pad_s, valid_s, pad_v, valid_v, w_in_ref, w_gate_ref, w_out_ref, gain_ref, shift_ref,
    out_ref,
    send, got, prod, back, wt, gate, first, lay, lay2, big, lhs,
    send_sem, got_sem, back_send_sem, back_sem,
):
    H = nr * nc
    C = pair_ref.shape[-1]
    N = nr * 32
    my_r = lax.axis_index("row")
    my_c = lax.axis_index("col")
    me = my_r * nc + my_c

    def peer(s):
        dr = s // nc
        dc = s % nc
        r = (my_r + dr) % nr
        c = (my_c + dc) % nc
        return r, c

    barrier = pltpu.get_barrier_semaphore()

    def greet(s, carry):
        r, c = peer(s)
        pl.semaphore_signal(barrier, inc=1, device_id=(r, c), device_id_type=MESH)
        return carry

    lax.fori_loop(1, H, greet, 0)

    lane = lax.broadcasted_iota(jnp.int32, (1, 128), 1)
    low = lane < HALF
    sub_low = lax.broadcasted_iota(jnp.int32, (128, 1), 0) < HALF
    odd = my_c % 2

    def col_flags(ref):
        row = ref[pl.ds(my_c // 2, 1), :]
        turned = pltpu.roll(row, HALF, 1)
        lo = jnp.where(odd == 1, turned, row)
        hi = jnp.where(odd == 1, row, turned)
        return jnp.where(low, lo, hi)

    pad_cols = col_flags(pad_v)
    valid_cols = jnp.transpose(jnp.broadcast_to(col_flags(valid_v), (128, 128)))

    def pad_tile(i2):
        top = pad_s[my_r * 32 + i2].astype(F32)
        bottom = pad_s[my_r * 32 + T + i2].astype(F32)
        return jnp.where(low, top, bottom) * pad_cols

    def valid_tile(i2):
        top = valid_s[my_r * 32 + i2].astype(F32)
        bottom = valid_s[my_r * 32 + T + i2].astype(F32)
        return jnp.where(sub_low, top, bottom) * valid_cols

    def project(u, source):
        wt[...] = jnp.transpose(w_in_ref[u].astype(F32)).astype(BF16)
        gain = gain_ref[u, 0:1]
        shift = shift_ref[u, 0:1]
        q = 4

        def chunk(g, carry):
            i2 = g * q
            values = source(i2, q).astype(F32)
            center = jnp.mean(values, axis=-1, keepdims=True)
            centred = values - center
            variance = jnp.mean(centred * centred, axis=-1, keepdims=True)
            normed = (centred * lax.rsqrt(variance + EPS) * gain + shift).astype(BF16)
            gating = sigmoid(jnp.dot(normed, w_gate_ref[u], preferred_element_type=F32))
            gate[pl.ds(i2 * 128, q * 128), :] = gating
            mask = jnp.concatenate([pad_tile(i2 + t) for t in range(q)], axis=1)

            def block(b):
                return lax.dot_general(
                    wt[b * H:(b + 1) * H, :], normed, (((1,), (1,)), ((), ())), preferred_element_type=F32
                )

            left = sigmoid(block(2)) * block(0) * mask
            for t in range(q):
                lay[pl.ds(i2 + t, H, stride=T), :] = left[:, t * 128:(t + 1) * 128]
            right = sigmoid(block(3)) * block(1) * mask
            for t in range(q):
                lay2[pl.ds(i2 + t, H, stride=T), :] = right[:, t * 128:(t + 1) * 128]
            return carry

        lax.fori_loop(0, T // q, chunk, 0)
        hs = 8

        def pack(g, carry):
            a = lay[pl.ds(g * hs * T, hs * T), :].astype(BF16).reshape(hs, T, 128)
            b = lay2[pl.ds(g * hs * T, hs * T), :].astype(BF16).reshape(hs, T, 128)
            send[pl.ds(g * hs, hs), 0] = a
            send[pl.ds(g * hs, hs), 1] = b
            return carry

        lax.fori_loop(0, H // hs, pack, 0)

    def exchange(source, target, s_sem, r_sem):
        own = pltpu.make_async_copy(source.at[me], target.at[me], r_sem)
        own.start()

        def go(s, carry):
            r, c = peer(s)
            pltpu.make_async_remote_copy(
                src_ref=source.at[r * nc + c], dst_ref=target.at[me], send_sem=s_sem, recv_sem=r_sem,
                device_id=(r, c), device_id_type=MESH,
            ).start()
            return carry

        lax.fori_loop(1, H, go, 0)

    def arrive(target, r_sem):
        pltpu.make_async_copy(target, target, r_sem).wait()

    def sent(source, s_sem):
        part = source.at[pl.ds(0, H - 1)]
        pltpu.make_async_copy(part, part, s_sem).wait()

    def halves(tile):
        turned = pltpu.roll(tile, HALF, 1)
        zero = jnp.zeros_like(tile)
        return (
            (jnp.where(low, tile, zero).astype(BF16), jnp.where(low, turned, zero).astype(BF16)),
            (jnp.where(low, zero, turned).astype(BF16), jnp.where(low, zero, tile).astype(BF16)),
        )

    def store_product(u, c0, width, value):
        for c in range(width):
            part = value[:, c * 128:(c + 1) * 128].astype(BF16).reshape(nr, T, 128)
            for r in range(nr):
                prod[u, r * nc + c0 + c] = part[r]

    def outgoing(u):
        box = got.at[u]
        for c in range(nc):
            for r in range(nr):
                lhs[r * T:(r + 1) * T, c * 128:(c + 1) * 128] = box[r * nc + c, 0]

        def build(r, carry):
            for c in range(nc):
                parts = halves(box[r * nc + c, 1].astype(F32))
                for ip in range(2):
                    for jp in range(2):
                        at = (r // 2) * 128 + ip * HALF + (r % 2) * 32 + jp * T
                        big[pl.ds(at, T), c * 128:(c + 1) * 128] = parts[ip][jp]
            return carry

        lax.fori_loop(0, nr, build, 0)
        for c in range(0, nc, 2):
            value = lax.dot_general(
                lhs[...], big[c * 128:(c + 2) * 128, :], (((1,), (1,)), ((), ())), preferred_element_type=F32
            )
            store_product(u, c, 2, value)

    def incoming(u):
        box = got.at[u]
        for c in range(nc):
            block = jnp.concatenate([box[r * nc + c, 0] for r in range(nr)], axis=0)
            turned = jnp.transpose(block.astype(F32)).astype(BF16)
            for kp in range(2):
                for hi in range(2):
                    for ip in range(2):
                        src = ((kp * 2 + hi) * 2 + ip) * T
                        dst = (c * 2 + hi) * T
                        at = (ip * 2 + kp) * nr * T
                        lhs[dst:dst + T, at:at + nr * T] = turned[src:src + T, :]

        def build(r, carry):
            for c in range(nc):
                parts = halves(box[r * nc + c, 1].astype(F32))
                for ip in range(2):
                    for kp in range(2):
                        at = (ip * 2 + kp) * nr * T + r * T
                        big[pl.ds(at, T), c * 128:(c + 1) * 128] = parts[ip][kp]
            return carry

        lax.fori_loop(0, nr, build, 0)
        for c in range(0, nc, 2):
            value = jnp.dot(lhs[...], big[:, c * 128:(c + 2) * 128], preferred_element_type=F32)
            store_product(u, c, 2, value)

    def finish(u, source, emit):
        q = 4
        hs = 8
        box = back.at[u]

        def widen(g, total):
            part = box[pl.ds(g * hs, hs)].astype(F32)
            lay[pl.ds(g * hs * T, hs * T), :] = part.reshape(hs * T, 128)
            return total

        lax.fori_loop(0, H // hs, widen, 0)
        gain = jnp.transpose(jnp.broadcast_to(gain_ref[u, 1:2, :H], (128, H)))
        shift = jnp.transpose(jnp.broadcast_to(shift_ref[u, 1:2, :H], (128, H)))

        def chunk(g, carry):
            i2 = g * q
            for t in range(q):
                mixed = lay[pl.ds(i2 + t, H, stride=T), :]
                center = jnp.mean(mixed, axis=0, keepdims=True)
                centred = mixed - center
                variance = jnp.mean(centred * centred, axis=0, keepdims=True)
                normed = centred * lax.rsqrt(variance + EPS) * gain + shift
                normed = jnp.transpose(normed).astype(BF16)
                update = jnp.dot(normed, w_out_ref[u], preferred_element_type=F32)
                gating = gate[pl.ds((i2 + t) * 128, 128), :]
                value = source(i2 + t, 1).astype(F32) + gating * update * valid_tile(i2 + t)
                emit(i2 + t, value.astype(BF16))
            return carry

        lax.fori_loop(0, T // q, chunk, 0)

    def from_pair(i2, q):
        top = pair_ref[pl.ds(i2, q)]
        bottom = pair_ref[pl.ds(i2 + T, q)]
        return jnp.concatenate([top, bottom], axis=1).reshape(q * 128, C)

    def from_first(i2, q):
        return first[pl.ds(i2, q)].reshape(q * 128, C)

    def to_first(i2, value):
        first[i2] = value

    def to_out(i2, value):
        out_ref[i2] = value[:HALF]
        out_ref[i2 + T] = value[HALF:]

    for u in range(2):
        source = from_pair if u == 0 else from_first
        project(u, source)
        if u == 0:
            pl.semaphore_wait(barrier, H - 1)
        exchange(send, got.at[u], send_sem.at[u], got_sem.at[u])
        arrive(got.at[u], got_sem.at[u])
        if u == 0:
            outgoing(u)
        else:
            incoming(u)
        exchange(prod.at[u], back.at[u], back_send_sem.at[u], back_sem.at[u])
        sent(send, send_sem.at[u])
        arrive(back.at[u], back_sem.at[u])
        finish(u, source, to_first if u == 0 else to_out)
    for u in range(2):
        sent(prod.at[u], back_send_sem.at[u])


def solution(mesh):
    nr, nc = mesh.shape["row"], mesh.shape["col"]

    def local(pair, pad_mask, valid_flags, w_in, w_gate, w_out, gains, shifts):
        H = nr * nc
        C = pair.shape[-1]
        vmem = pl.BlockSpec(memory_space=pltpu.VMEM)
        smem = pl.BlockSpec(memory_space=pltpu.SMEM)
        pad_v = pad_mask.astype(F32).reshape(-1, 128)
        valid_v = valid_flags.astype(F32).reshape(-1, 128)
        return pl.pallas_call(
            functools.partial(kernel, nr, nc),
            out_shape=jax.ShapeDtypeStruct(pair.shape, BF16),
            in_specs=[vmem, smem, smem] + [vmem] * 7,
            out_specs=vmem,
            scratch_shapes=[
                pltpu.VMEM((H, 2, T, 128), BF16),
                pltpu.VMEM((2, H, 2, T, 128), BF16),
                pltpu.VMEM((2, H, T, 128), BF16),
                pltpu.VMEM((2, H, T, 128), BF16),
                pltpu.VMEM((4 * H, C), BF16),
                pltpu.VMEM((T * 128, C), F32),
                pltpu.VMEM((T, 128, C), BF16),
                pltpu.VMEM((H * T, 128), F32),
                pltpu.VMEM((H * T, 128), F32),
                pltpu.VMEM((nc * 128, nc * 128), BF16),
                pltpu.VMEM((nr * T, nc * 128), BF16),
                pltpu.SemaphoreType.DMA((2,)),
                pltpu.SemaphoreType.DMA((2,)),
                pltpu.SemaphoreType.DMA((2,)),
                pltpu.SemaphoreType.DMA((2,)),
            ],
            compiler_params=pltpu.CompilerParams(
                collective_id=0, has_side_effects=True, vmem_limit_bytes=48 * 1024 * 1024
            ),
        )(pair, pad_mask, valid_flags, pad_v, valid_v, w_in, w_gate, w_out, gains, shifts)

    placed = (P("row", "col", None), P(), P(), P(), P(), P(), P(), P())
    return jax.shard_map(
        local, mesh=mesh, in_specs=placed, out_specs=P("row", "col", None), check_vma=False
    )
```

```python
import functools
import itertools

import jax
import jax.numpy as jnp
from jax import lax
from jax.experimental import pallas as pl
from jax.experimental.pallas import tpu as pltpu
from jax.sharding import PartitionSpec as P

EPS = 1e-05
MESH = pl.DeviceIdType.MESH
F32 = jnp.float32
BF16 = jnp.bfloat16
T = 16
HALF = 64
NN = (((1,), (0,)), ((), ()))
NT = (((1,), (1,)), ((), ()))


def sigmoid(v):
    return 0.5 * jnp.tanh(0.5 * v) + 0.5


def dot(a, b, dims=NN):
    return lax.dot_general(a, b, dims, preferred_element_type=F32)


def hops(shift, size):
    return min(shift, size - shift)


def kernel(
    nr, nc, pair_hbm, pad_hbm, valid_hbm, w_in_hbm, w_gate_hbm, w_out_hbm, gain_hbm, shift_hbm,
    out_hbm,
    pair_ref, pad_v, valid_v, w_in_ref, w_gate_ref, w_out_ref, gain_ref, shift_ref, pad_s, valid_s, out_ref,
    send, got, prod, back, wt, nb, gate, first, lay, big, lhs,
    load_sem, send_sem, got_sem, back_send_sem, back_sem, out_sem,
):
    H = nr * nc
    C = pair_ref.shape[-1]
    X, Y = nr // 4, nc // 2
    my_r = lax.axis_index("row")
    my_c = lax.axis_index("col")
    me = my_r * nc + my_c

    xs = [(my_r // 4 + d) % X for d in range(X)]
    ys = [(my_c // 2 + d) % Y for d in range(Y)]
    zs = [((my_c % 2) * 2 + (my_r // 2) % 2 + d) % 4 for d in range(4)]
    ks = [(my_r % 2 + d) % 2 for d in range(2)]
    row_parts = [[xs[dx] * 4 + ks[dk] for dk in range(2)] for dx in range(X)]
    z_lo = [(z % 2) * 2 for z in zs]
    z_hi = [z // 2 for z in zs]

    def peer(shift):
        dx, dy, dz, dk = shift
        return row_parts[dx][dk] + z_lo[dz], ys[dy] * 2 + z_hi[dz]

    def distance(shift):
        dx, dy, dz, dk = shift
        return hops(dx, X) + hops(dy, Y) + hops(dz, 4) + 0.3 * dk

    here = (0, 0, 0, 0)
    shifts = [s for s in itertools.product(range(X), range(Y), range(4), range(2)) if s != here]
    shifts.sort(key=lambda s: -distance(s))

    loads = []
    for i, (a, b) in enumerate((
        (pair_hbm, pair_ref), (w_in_hbm, w_in_ref), (gain_hbm, gain_ref), (shift_hbm, shift_ref), (pad_hbm, pad_v),
        (pad_hbm, pad_s), (w_gate_hbm, w_gate_ref), (w_out_hbm, w_out_ref), (valid_hbm, valid_v),
        (valid_hbm, valid_s),
    )):
        copy = pltpu.make_async_copy(a, b, load_sem.at[i])
        copy.start()
        loads.append(copy)

    barrier = pltpu.get_barrier_semaphore()
    for s in shifts:
        pl.semaphore_signal(barrier, inc=1, device_id=peer(s), device_id_type=MESH)

    lane = lax.broadcasted_iota(jnp.int32, (1, 128), 1)
    low = lane < HALF
    sub_low = lax.broadcasted_iota(jnp.int32, (128, 1), 0) < HALF
    odd = my_c % 2

    def col_flags(ref):
        row = ref[pl.ds(my_c // 2, 1), :].astype(F32)
        turned = pltpu.roll(row, HALF, 1)
        lo = jnp.where(odd == 1, turned, row)
        hi = jnp.where(odd == 1, row, turned)
        return jnp.where(low, lo, hi)

    def flag(ref, i):
        return ref[i // 128, i % 128].astype(F32)

    def pad_tile(cols, i2):
        top = flag(pad_s, my_r * 32 + i2)
        bottom = flag(pad_s, my_r * 32 + T + i2)
        return jnp.where(low, top, bottom) * cols

    def valid_tile(cols, i2):
        top = flag(valid_s, my_r * 32 + i2)
        bottom = flag(valid_s, my_r * 32 + T + i2)
        return jnp.where(sub_low, top, bottom) * cols

    def turn_weights(u):
        wt[u] = jnp.transpose(w_in_ref[u].astype(F32)).astype(BF16)

    q = 4

    def normalize(u, source):
        gain = gain_ref[u, 0:1]
        shift = shift_ref[u, 0:1]

        def chunk(g, carry):
            values = source(g * q, q).astype(F32)
            center = jnp.mean(values, axis=-1, keepdims=True)
            centred = values - center
            variance = jnp.mean(centred * centred, axis=-1, keepdims=True)
            normed = centred * lax.rsqrt(variance + EPS) * gain + shift
            nb[pl.ds(g * q * 128, q * 128), :] = normed.astype(BF16)
            return carry

        lax.fori_loop(0, T // q, chunk, 0)

    def project(u, side):
        cols = col_flags(pad_v)

        def chunk(g, carry):
            normed = nb[pl.ds(g * q * 128, q * 128), :]
            mask = jnp.concatenate([pad_tile(cols, g * q + t) for t in range(q)], axis=1)
            value = dot(wt[u, side * H:(side + 1) * H, :], normed, NT)
            scale = sigmoid(dot(wt[u, (2 + side) * H:(3 + side) * H, :], normed, NT)) * mask
            value = value * scale
            for t in range(q):
                lay[pl.ds(g * q + t, H, stride=T), :] = value[:, t * 128:(t + 1) * 128]
            return carry

        lax.fori_loop(0, T // q, chunk, 0)
        hs = 8

        def pack(g, carry):
            send[u, side, pl.ds(g * hs, hs)] = (
                lay[pl.ds(g * hs * T, hs * T), :].astype(BF16).reshape(hs, T, 128)
            )
            return carry

        lax.fori_loop(0, H // hs, pack, 0)

    def gates(u):
        def chunk(g, carry):
            rows = pl.ds(g * q * 128, q * 128)
            gate[rows, :] = sigmoid(dot(nb[rows, :], w_gate_ref[u]))
            return carry

        lax.fori_loop(0, T // q, chunk, 0)

    def put(source, target, s_sem, r_sem, some):
        for s in some:
            if s == here:
                pltpu.make_async_copy(source.at[me], target.at[me], r_sem).start()
            else:
                r, c = peer(s)
                pltpu.make_async_remote_copy(
                    src_ref=source.at[r * nc + c], dst_ref=target.at[me], send_sem=s_sem, recv_sem=r_sem,
                    device_id=(r, c), device_id_type=MESH,
                ).start()

    def arrive(target, r_sem):
        pltpu.make_async_copy(target, target, r_sem).wait()

    def sent(source, s_sem):
        part = source.at[pl.ds(0, H - 1)]
        pltpu.make_async_copy(part, part, s_sem).wait()

    def halves(tile):
        turned = pltpu.roll(tile, HALF, 1)
        zero = jnp.zeros_like(tile)
        return (
            (jnp.where(low, tile, zero).astype(BF16), jnp.where(low, turned, zero).astype(BF16)),
            (jnp.where(low, zero, turned).astype(BF16), jnp.where(low, zero, tile).astype(BF16)),
        )

    def build(u):
        box = got.at[u, 1]

        def step(r, carry):
            for c in range(nc):
                parts = halves(box[r * nc + c].astype(F32))
                for ip in range(2):
                    for p in range(2):
                        if u == 0:
                            at = (r // 2) * 128 + ip * HALF + (r % 2) * 32 + p * T
                        else:
                            at = (ip * 2 + p) * nr * T + r * T
                        big[pl.ds(pl.multiple_of(at, T), T), c * 128:(c + 1) * 128] = parts[ip][p]
            return carry

        lax.fori_loop(0, nr, step, 0)

    def line_up(u):
        box = got.at[u, 0]
        for c in range(nc):
            if u == 0:
                for r in range(nr):
                    lhs[r * T:(r + 1) * T, c * 128:(c + 1) * 128] = box[r * nc + c]
            else:
                block = jnp.concatenate([box[r * nc + c] for r in range(nr)], axis=0)
                turned = jnp.transpose(block.astype(F32)).astype(BF16)
                for kp, hi, ip in itertools.product(range(2), range(2), range(2)):
                    src = ((kp * 2 + hi) * 2 + ip) * T
                    dst = (c * 2 + hi) * T
                    at = (ip * 2 + kp) * nr * T
                    lhs[dst:dst + T, at:at + nr * T] = turned[src:src + T, :]

    def contract(u):
        for dy in sorted(range(Y), key=lambda d: -hops(d, Y)):
            c0 = ys[dy] * 2
            span = pl.ds(pl.multiple_of(c0 * 128, 256), 256)
            if u == 0:
                value = dot(lhs[...], big[span, :], NT)
            else:
                value = dot(lhs[...], big[:, span])
            for c in range(2):
                part = value[:, c * 128:(c + 1) * 128].astype(BF16).reshape(nr, T, 128)
                for r in range(nr):
                    prod[u, r * nc + c0 + c] = part[r]
            some = [s for s in shifts + [here] if s[1] == dy]
            put(prod.at[u], back.at[u], back_send_sem.at[u], back_sem.at[u], some)

    def finish(u, source, emit):
        hs = 8
        box = back.at[u]

        def widen(g, carry):
            part = box[pl.ds(g * hs, hs)].astype(F32)
            lay[pl.ds(g * hs * T, hs * T), :] = part.reshape(hs * T, 128)
            return carry

        gain = jnp.transpose(jnp.broadcast_to(gain_ref[u, 1:2, :H], (128, H)))
        shift = jnp.transpose(jnp.broadcast_to(shift_ref[u, 1:2, :H], (128, H)))
        cols = jnp.transpose(jnp.broadcast_to(col_flags(valid_v), (128, 128)))
        arrive(box, back_sem.at[u])
        lax.fori_loop(0, H // hs, widen, 0)

        def chunk(g, carry):
            i2 = g * q
            for t in range(q):
                mixed = lay[pl.ds(i2 + t, H, stride=T), :]
                center = jnp.mean(mixed, axis=0, keepdims=True)
                centred = mixed - center
                variance = jnp.mean(centred * centred, axis=0, keepdims=True)
                normed = centred * lax.rsqrt(variance + EPS) * gain + shift
                normed = jnp.transpose(normed).astype(BF16)
                update = dot(normed, w_out_ref[u])
                gating = gate[pl.ds((i2 + t) * 128, 128), :]
                value = source(i2 + t, 1).astype(F32) + gating * update * valid_tile(cols, i2 + t)
                emit(i2 + t, value.astype(BF16))
            return carry

        lax.fori_loop(0, T // q, chunk, 0)

    def from_pair(i2, n):
        top = pair_ref[pl.ds(i2, n)]
        bottom = pair_ref[pl.ds(i2 + T, n)]
        return jnp.concatenate([top, bottom], axis=1).reshape(n * 128, C)

    def from_first(i2, n):
        return first[pl.ds(i2, n)].reshape(n * 128, C)

    def to_first(i2, value):
        first[i2] = value

    def to_out(i2, value):
        out_ref[i2] = value[:HALF]
        out_ref[i2 + T] = value[HALF:]

    for copy in loads[:6]:
        copy.wait()
    turn_weights(0)
    for u in range(2):
        source = from_pair if u == 0 else from_first
        normalize(u, source)
        project(u, 1)
        if u == 0:
            pl.semaphore_wait(barrier, H - 1)
        for side in (1, 0):
            if side == 0:
                project(u, 0)
            put(send.at[u, side], got.at[u, side], send_sem.at[u, side], got_sem.at[u, side], shifts + [here])
        if u == 0:
            for copy in loads[6:]:
                copy.wait()
        gates(u)
        if u == 0:
            turn_weights(1)
        arrive(got.at[u, 1], got_sem.at[u, 1])
        build(u)
        arrive(got.at[u, 0], got_sem.at[u, 0])
        line_up(u)
        contract(u)
        finish(u, source, to_first if u == 0 else to_out)
    last = pltpu.make_async_copy(out_ref, out_hbm, out_sem)
    last.start()
    for u in range(2):
        for side in range(2):
            sent(send.at[u, side], send_sem.at[u, side])
        sent(prod.at[u], back_send_sem.at[u])
    last.wait()


def solution(mesh):
    nr, nc = mesh.shape["row"], mesh.shape["col"]

    def local(pair, pad_mask, valid_flags, w_in, w_gate, w_out, gains, shifts):
        H = nr * nc
        C = pair.shape[-1]
        hbm = pl.BlockSpec(memory_space=pl.ANY)
        pad_mask = pad_mask.reshape(-1, 128)
        valid_flags = valid_flags.reshape(-1, 128)
        operands = (pair, pad_mask, valid_flags, w_in, w_gate, w_out, gains, shifts)
        dma = pltpu.SemaphoreType.DMA
        return pl.pallas_call(
            functools.partial(kernel, nr, nc),
            out_shape=jax.ShapeDtypeStruct(pair.shape, BF16),
            in_specs=[hbm] * len(operands),
            out_specs=hbm,
            scratch_shapes=[pltpu.VMEM(a.shape, a.dtype) for a in operands] + [
                pltpu.SMEM(pad_mask.shape, pad_mask.dtype),
                pltpu.SMEM(valid_flags.shape, valid_flags.dtype),
                pltpu.VMEM(pair.shape, BF16),
                pltpu.VMEM((2, 2, H, T, 128), BF16),
                pltpu.VMEM((2, 2, H, T, 128), BF16),
                pltpu.VMEM((2, H, T, 128), BF16),
                pltpu.VMEM((2, H, T, 128), BF16),
                pltpu.VMEM((2, 4 * H, C), BF16),
                pltpu.VMEM((T * 128, C), BF16),
                pltpu.VMEM((T * 128, C), F32),
                pltpu.VMEM((T, 128, C), BF16),
                pltpu.VMEM((H * T, 128), F32),
                pltpu.VMEM((nc * 128, nc * 128), BF16),
                pltpu.VMEM((nr * T, nc * 128), BF16),
                dma((10,)), dma((2, 2)), dma((2, 2)), dma((2,)), dma((2,)), dma,
            ],
            compiler_params=pltpu.CompilerParams(
                collective_id=0, has_side_effects=True, vmem_limit_bytes=48 * 1024 * 1024
            ),
        )(*operands)

    placed = (P("row", "col", None), P(), P(), P(), P(), P(), P(), P())
    return jax.shard_map(
        local, mesh=mesh, in_specs=placed, out_specs=P("row", "col", None), check_vma=False
    )
```

```python
import functools
import itertools

import jax
import jax.numpy as jnp
from jax import lax
from jax.experimental import pallas as pl
from jax.experimental.pallas import tpu as pltpu
from jax.sharding import PartitionSpec as P

EPS = 1e-05
MESH = pl.DeviceIdType.MESH
F32 = jnp.float32
BF16 = jnp.bfloat16
T = 16
HALF = 64
NN = (((1,), (0,)), ((), ()))
NT = (((1,), (1,)), ((), ()))


def sigmoid(v):
    return 0.5 * jnp.tanh(0.5 * v) + 0.5


def dot(a, b, dims=NN):
    return lax.dot_general(a, b, dims, preferred_element_type=F32)


def hops(shift, size):
    return min(shift, size - shift)


def kernel(
    nr, nc, pair_hbm, pad_hbm, valid_hbm, w_in_hbm, w_gate_hbm, w_out_hbm, gain_hbm, shift_hbm,
    out_hbm,
    pair_ref, pad_v, valid_v, w_in_ref, w_gate_ref, w_out_ref, gain_ref, shift_ref, pad_s, valid_s, out_ref,
    send, got, prod, back, wt, nb, gate, first, lay, lay2, big, lhs,
    load_sem, send_sem, got_sem, back_send_sem, back_sem, out_sem,
):
    H = nr * nc
    C = pair_ref.shape[-1]
    X, Y = nr // 4, nc // 2
    my_r = lax.axis_index("row")
    my_c = lax.axis_index("col")
    me = my_r * nc + my_c

    xs = [(my_r // 4 + d) % X for d in range(X)]
    ys = [(my_c // 2 + d) % Y for d in range(Y)]
    zs = [((my_c % 2) * 2 + (my_r // 2) % 2 + d) % 4 for d in range(4)]
    ks = [(my_r % 2 + d) % 2 for d in range(2)]
    row_parts = [[xs[dx] * 4 + ks[dk] for dk in range(2)] for dx in range(X)]
    z_lo = [(z % 2) * 2 for z in zs]
    z_hi = [z // 2 for z in zs]

    def peer(shift):
        dx, dy, dz, dk = shift
        return row_parts[dx][dk] + z_lo[dz], ys[dy] * 2 + z_hi[dz]

    def distance(shift):
        dx, dy, dz, dk = shift
        return hops(dx, X) + hops(dy, Y) + hops(dz, 4) + 0.3 * dk

    here = (0, 0, 0, 0)
    shifts = [s for s in itertools.product(range(X), range(Y), range(4), range(2)) if s != here]
    shifts.sort(key=lambda s: -distance(s))

    loads = []
    for i, (a, b) in enumerate((
        (pair_hbm, pair_ref), (w_in_hbm, w_in_ref), (gain_hbm, gain_ref), (shift_hbm, shift_ref), (pad_hbm, pad_v),
        (pad_hbm, pad_s), (w_gate_hbm, w_gate_ref), (w_out_hbm, w_out_ref), (valid_hbm, valid_v),
        (valid_hbm, valid_s),
    )):
        copy = pltpu.make_async_copy(a, b, load_sem.at[i])
        copy.start()
        loads.append(copy)

    barrier = pltpu.get_barrier_semaphore()
    for s in shifts:
        pl.semaphore_signal(barrier, inc=1, device_id=peer(s), device_id_type=MESH)

    lane = lax.broadcasted_iota(jnp.int32, (1, 128), 1)
    low = lane < HALF
    sub_low = lax.broadcasted_iota(jnp.int32, (128, 1), 0) < HALF
    odd = my_c % 2

    def col_flags(ref):
        row = ref[pl.ds(my_c // 2, 1), :].astype(F32)
        turned = pltpu.roll(row, HALF, 1)
        lo = jnp.where(odd == 1, turned, row)
        hi = jnp.where(odd == 1, row, turned)
        return jnp.where(low, lo, hi)

    def flag(ref, i):
        return ref[i // 128, i % 128].astype(F32)

    def pad_tile(cols, i2):
        top = flag(pad_s, my_r * 32 + i2)
        bottom = flag(pad_s, my_r * 32 + T + i2)
        return jnp.where(low, top, bottom) * cols

    def valid_tile(cols, i2):
        top = flag(valid_s, my_r * 32 + i2)
        bottom = flag(valid_s, my_r * 32 + T + i2)
        return jnp.where(sub_low, top, bottom) * cols

    def turn_weights(u):
        wt[u] = jnp.transpose(w_in_ref[u].astype(F32)).astype(BF16)

    q = 4
    B = T // 2

    def normalize(u, i2, values):
        values = values.astype(F32)
        center = jnp.mean(values, axis=-1, keepdims=True)
        centred = values - center
        variance = jnp.mean(centred * centred, axis=-1, keepdims=True)
        normed = centred * lax.rsqrt(variance + EPS) * gain_ref[u, 0:1] + shift_ref[u, 0:1]
        normed = normed.astype(BF16)
        nb[pl.ds(i2 * 128, q * 128), :] = normed
        return normed

    def project(u, side, normed, mask, at):
        value = dot(wt[u, side * H:(side + 1) * H, :], normed, NT)
        value = value * (sigmoid(dot(wt[u, (2 + side) * H:(3 + side) * H, :], normed, NT)) * mask)
        for t in range(q):
            lay[pl.ds(at + t, H, stride=T), :] = value[:, t * 128:(t + 1) * 128]

    def pad_mask(cols, i2):
        return jnp.concatenate([pad_tile(cols, i2 + t) for t in range(q)], axis=1)

    def pack(target):
        hs = min(16, H)

        def some(g, carry):
            target[pl.ds(g * hs, hs)] = lay[pl.ds(g * hs * T, hs * T), :].astype(BF16).reshape(hs, T, 128)
            return carry

        for_each(H // hs, some)

    def for_each(n, step):
        if n:
            lax.fori_loop(0, n, step, 0)

    def gates(u):
        def chunk(g, carry):
            rows = pl.ds(g * q * 128, q * 128)
            gate[rows, :] = sigmoid(dot(nb[rows, :], w_gate_ref[u]))
            return carry

        for_each(T // q, chunk)

    def put(source, target, s_sem, r_sem, some):
        for s in some:
            if s == here:
                pltpu.make_async_copy(source.at[me], target.at[me], r_sem).start()
            else:
                r, c = peer(s)
                pltpu.make_async_remote_copy(
                    src_ref=source.at[r * nc + c], dst_ref=target.at[me], send_sem=s_sem, recv_sem=r_sem,
                    device_id=(r, c), device_id_type=MESH,
                ).start()

    def put_block(u, part):
        put(send.at[u, part], got.at[u, part], send_sem.at[u, part], got_sem.at[u, part], shifts + [here])

    def put_back(u, half, some):
        put(prod.at[u, half], back.at[u, half], back_send_sem.at[u, half], back_sem.at[u, half], some)

    def arrive(target, r_sem):
        pltpu.make_async_copy(target, target, r_sem).wait()

    def sent(source, s_sem):
        part = source.at[pl.ds(0, H - 1)]
        pltpu.make_async_copy(part, part, s_sem).wait()

    def halves(tile):
        turned = pltpu.roll(tile, HALF, 1)
        zero = jnp.zeros_like(tile)
        return (
            (jnp.where(low, tile, zero).astype(BF16), jnp.where(low, turned, zero).astype(BF16)),
            (jnp.where(low, zero, turned).astype(BF16), jnp.where(low, zero, tile).astype(BF16)),
        )

    def build_outgoing():
        box = got.at[0, 1]

        def step(r, carry):
            for c in range(nc):
                parts = halves(box[r * nc + c].astype(F32))
                for ip in range(2):
                    for p in range(2):
                        at = (r // 2) * 128 + ip * HALF + (r % 2) * 32 + p * T
                        big[pl.ds(pl.multiple_of(at, T), T), c * 128:(c + 1) * 128] = parts[ip][p]
            return carry

        for_each(nr, step)

    def line_up_outgoing():
        box = got.at[0, 0]
        for c in range(nc):
            for r in range(nr):
                lhs[r * T:(r + 1) * T, c * 128:(c + 1) * 128] = box[r * nc + c]

    def build_incoming(half):
        box = got.at[1, half]

        def step(g, carry):
            r = g * 2
            for c in range(nc):
                tile = jnp.concatenate(
                    [box[r * nc + c].astype(F32)[:B], box[(r + 1) * nc + c].astype(F32)[:B]], axis=0
                )
                parts = halves(tile)
                for ip in range(2):
                    for p in range(2):
                        at = ((ip * 2 + p) * 2 + half) * nr * B + g * T
                        big[pl.ds(pl.multiple_of(at, T), T), c * 128:(c + 1) * 128] = parts[ip][p]
            return carry

        for_each(nr // 2, step)

    def line_up_incoming(half):
        box = got.at[1, half]
        for c in range(nc):
            block = jnp.concatenate([box[r * nc + c].astype(F32)[B:] for r in range(nr)], axis=0)
            turned = jnp.transpose(block).astype(BF16)
            for kp, hi, ip in itertools.product(range(2), range(2), range(2)):
                src = ((kp * 2 + hi) * 2 + ip) * T
                dst = (c * 2 + hi) * T
                at = ((ip * 2 + kp) * 2 + half) * nr * B
                lhs[dst:dst + T, at:at + nr * B] = turned[src:src + T, :]

    def contract(u):
        for dy in sorted(range(Y), key=lambda d: -hops(d, Y)):
            c0 = ys[dy] * 2
            span = pl.ds(pl.multiple_of(c0 * 128, 256), 256)
            if u == 0:
                value = dot(lhs[...], big[span, :], NT)
            else:
                value = dot(lhs[...], big[:, span])
            for c in range(2):
                part = value[:, c * 128:(c + 1) * 128].astype(BF16).reshape(nr, 2, B, 128)
                for r in range(nr):
                    for half in range(2):
                        prod[u, half, r * nc + c0 + c] = part[r, half]
            put_back(u, 0, [s for s in shifts + [here] if s[1] == dy])
        put_back(u, 1, shifts + [here])

    def finish_start(u):
        gain = jnp.transpose(jnp.broadcast_to(gain_ref[u, 1:2, :H], (128, H)))
        shift = jnp.transpose(jnp.broadcast_to(shift_ref[u, 1:2, :H], (128, H)))
        cols = jnp.transpose(jnp.broadcast_to(col_flags(valid_v), (128, 128)))
        return gain, shift, cols

    def widen(u, half):
        hs = min(16, H)
        box = back.at[u, half]
        arrive(box, back_sem.at[u, half])

        def some(g, carry):
            lay2[pl.ds(g * hs * B, hs * B), :] = box[pl.ds(g * hs, hs)].astype(F32).reshape(hs * B, 128)
            return carry

        for_each(H // hs, some)

    def finish(u, half, row, factors, old):
        gain, shift, cols = factors
        i2 = half * B + row
        mixed = lay2[pl.ds(row, H, stride=B), :]
        center = jnp.mean(mixed, axis=0, keepdims=True)
        centred = mixed - center
        variance = jnp.mean(centred * centred, axis=0, keepdims=True)
        normed = centred * lax.rsqrt(variance + EPS) * gain + shift
        normed = jnp.transpose(normed).astype(BF16)
        update = dot(normed, w_out_ref[u])
        gating = gate[pl.ds(i2 * 128, 128), :]
        return (old.astype(F32) + gating * update * valid_tile(cols, i2)).astype(BF16)

    def from_pair(i2, n):
        top = pair_ref[pl.ds(i2, n)]
        bottom = pair_ref[pl.ds(i2 + T, n)]
        return jnp.concatenate([top, bottom], axis=1).reshape(n * 128, C)

    for copy in loads[:6]:
        copy.wait()
    turn_weights(0)
    pad_cols = col_flags(pad_v)

    def right_first(g, carry):
        i2 = g * q
        normed = normalize(0, i2, from_pair(i2, q))
        project(0, 1, normed, pad_mask(pad_cols, i2), i2)
        return carry

    def left_next(g, carry):
        i2 = g * q
        project(0, 0, nb[pl.ds(i2 * 128, q * 128), :], pad_mask(pad_cols, i2), i2)
        return carry

    for_each(T // q, right_first)
    pack(send.at[0, 1])
    pl.semaphore_wait(barrier, H - 1)
    put_block(0, 1)
    for_each(T // q, left_next)
    pack(send.at[0, 0])
    put_block(0, 0)
    for copy in loads[6:]:
        copy.wait()
    gates(0)
    turn_weights(1)
    factors = finish_start(0)
    arrive(got.at[0, 1], got_sem.at[0, 1])
    build_outgoing()
    arrive(got.at[0, 0], got_sem.at[0, 0])
    line_up_outgoing()
    contract(0)

    for half in range(2):
        widen(0, half)

        def middle(g, carry, half=half):
            i2 = half * B + g * q
            values = []
            for t in range(q):
                value = finish(0, half, g * q + t, factors, from_pair(i2 + t, 1))
                first[i2 + t] = value
                values.append(value)
            normed = normalize(1, i2, jnp.concatenate(values, axis=0))
            mask = pad_mask(pad_cols, i2)
            project(1, 1, normed, mask, g * q)
            project(1, 0, normed, mask, B + g * q)
            return carry

        for_each(B // q, middle)
        pack(send.at[1, half])
        put_block(1, half)
    gates(1)
    factors = finish_start(1)
    for half in range(2):
        arrive(got.at[1, half], got_sem.at[1, half])
        build_incoming(half)
        line_up_incoming(half)
    contract(1)
    outs = []
    for half in range(2):
        widen(1, half)

        def end(g, carry, half=half):
            for t in range(q):
                i2 = half * B + g * q + t
                value = finish(1, half, g * q + t, factors, first[i2])
                out_ref[i2] = value[:HALF]
                out_ref[i2 + T] = value[HALF:]
            return carry

        for_each(B // q, end)
        for i, at in enumerate((half * B, T + half * B)):
            rows = pl.ds(at, B)
            copy = pltpu.make_async_copy(out_ref.at[rows], out_hbm.at[rows], out_sem.at[half * 2 + i])
            copy.start()
            outs.append(copy)
    for u in range(2):
        for part in range(2):
            sent(send.at[u, part], send_sem.at[u, part])
            sent(prod.at[u, part], back_send_sem.at[u, part])
    for copy in outs:
        copy.wait()


def solution(mesh):
    nr, nc = mesh.shape["row"], mesh.shape["col"]

    def local(pair, pad_mask, valid_flags, w_in, w_gate, w_out, gains, shifts):
        H = nr * nc
        C = pair.shape[-1]
        hbm = pl.BlockSpec(memory_space=pl.ANY)
        pad_mask = pad_mask.reshape(-1, 128)
        valid_flags = valid_flags.reshape(-1, 128)
        operands = (pair, pad_mask, valid_flags, w_in, w_gate, w_out, gains, shifts)
        dma = pltpu.SemaphoreType.DMA
        return pl.pallas_call(
            functools.partial(kernel, nr, nc),
            out_shape=jax.ShapeDtypeStruct(pair.shape, BF16),
            in_specs=[hbm] * len(operands),
            out_specs=hbm,
            scratch_shapes=[pltpu.VMEM(a.shape, a.dtype) for a in operands] + [
                pltpu.SMEM(pad_mask.shape, pad_mask.dtype),
                pltpu.SMEM(valid_flags.shape, valid_flags.dtype),
                pltpu.VMEM(pair.shape, BF16),
                pltpu.VMEM((2, 2, H, T, 128), BF16),
                pltpu.VMEM((2, 2, H, T, 128), BF16),
                pltpu.VMEM((2, 2, H, T // 2, 128), BF16),
                pltpu.VMEM((2, 2, H, T // 2, 128), BF16),
                pltpu.VMEM((2, 4 * H, C), BF16),
                pltpu.VMEM((T * 128, C), BF16),
                pltpu.VMEM((T * 128, C), F32),
                pltpu.VMEM((T, 128, C), BF16),
                pltpu.VMEM((H * T, 128), F32),
                pltpu.VMEM((H * T // 2, 128), F32),
                pltpu.VMEM((nc * 128, nc * 128), BF16),
                pltpu.VMEM((nr * T, nc * 128), BF16),
                dma((10,)), dma((2, 2)), dma((2, 2)), dma((2, 2)), dma((2, 2)), dma((4,)),
            ],
            compiler_params=pltpu.CompilerParams(
                collective_id=0, has_side_effects=True, vmem_limit_bytes=60 * 1024 * 1024
            ),
        )(*operands)

    placed = (P("row", "col", None), P(), P(), P(), P(), P(), P(), P())
    return jax.shard_map(
        local, mesh=mesh, in_specs=placed, out_specs=P("row", "col", None), check_vma=False
    )
```

```python
import functools
import itertools

import jax
import jax.numpy as jnp
from jax import lax
from jax.experimental import pallas as pl
from jax.experimental.pallas import tpu as pltpu
from jax.sharding import PartitionSpec as P

EPS = 1e-05
MESH = pl.DeviceIdType.MESH
F32 = jnp.float32
BF16 = jnp.bfloat16
T = 16
HALF = 64
NN = (((1,), (0,)), ((), ()))
NT = (((1,), (1,)), ((), ()))


def sigmoid(v):
    return 0.5 * jnp.tanh(0.5 * v) + 0.5


def dot(a, b, dims=NN):
    return lax.dot_general(a, b, dims, preferred_element_type=F32)


def hops(shift, size):
    return min(shift, size - shift)


def kernel(
    nr, nc, pair_hbm, pad_hbm, valid_hbm, w_in_hbm, w_gate_hbm, w_out_hbm, gain_hbm, shift_hbm,
    out_hbm,
    pair_ref, pad_v, valid_v, w_in_ref, w_gate_ref, w_out_ref, gain_ref, shift_ref, pad_s, valid_s, out_ref,
    send, got, send_left, got_left, prod, back, wt, wg, wo, nb, gate, held, lay, lay2, big, lhs,
    load_sem, send_sem, got_sem, left_send_sem, left_sem, back_send_sem, back_sem, out_sem,
):
    H = nr * nc
    C = pair_ref.shape[-1]
    X, Y = nr // 4, nc // 2
    my_r = lax.axis_index("row")
    my_c = lax.axis_index("col")
    me = my_r * nc + my_c

    xs = [(my_r // 4 + d) % X for d in range(X)]
    ys = [(my_c // 2 + d) % Y for d in range(Y)]
    zs = [((my_c % 2) * 2 + (my_r // 2) % 2 + d) % 4 for d in range(4)]
    ks = [(my_r % 2 + d) % 2 for d in range(2)]
    row_parts = [[xs[dx] * 4 + ks[dk] for dk in range(2)] for dx in range(X)]
    z_lo = [(z % 2) * 2 for z in zs]
    z_hi = [z // 2 for z in zs]

    def peer(shift):
        dx, dy, dz, dk = shift
        return row_parts[dx][dk] + z_lo[dz], ys[dy] * 2 + z_hi[dz]

    def distance(shift):
        dx, dy, dz, dk = shift
        return hops(dx, X) + hops(dy, Y) + hops(dz, 4) + 0.3 * dk

    here = (0, 0, 0, 0)
    shifts = [s for s in itertools.product(range(X), range(Y), range(4), range(2)) if s != here]
    shifts.sort(key=lambda s: -distance(s))

    loads = []
    for i, (a, b) in enumerate((
        (pair_hbm, pair_ref), (w_in_hbm, w_in_ref), (gain_hbm, gain_ref), (shift_hbm, shift_ref), (pad_hbm, pad_v),
        (pad_hbm, pad_s), (w_gate_hbm, w_gate_ref), (w_out_hbm, w_out_ref), (valid_hbm, valid_v),
        (valid_hbm, valid_s),
    )):
        copy = pltpu.make_async_copy(a, b, load_sem.at[i])
        copy.start()
        loads.append(copy)

    barrier = pltpu.get_barrier_semaphore()
    for s in shifts:
        pl.semaphore_signal(barrier, inc=1, device_id=peer(s), device_id_type=MESH)

    lane = lax.broadcasted_iota(jnp.int32, (1, 128), 1)
    low = lane < HALF
    odd = my_c % 2

    def col_flags(ref):
        row = ref[pl.ds(my_c // 2, 1), :].astype(F32)
        turned = pltpu.roll(row, HALF, 1)
        lo = jnp.where(odd == 1, turned, row)
        hi = jnp.where(odd == 1, row, turned)
        return jnp.where(low, lo, hi)

    def flag(ref, i):
        return ref[i // 128, i % 128].astype(F32)

    q = 4
    B = T // 2

    def flags(ref, cols, i2):
        tiles = []
        for t in range(q):
            top = flag(ref, my_r * 32 + i2 + t)
            bottom = flag(ref, my_r * 32 + T + i2 + t)
            tiles.append(jnp.where(low, top, bottom) * cols)
        return jnp.concatenate(tiles, axis=1)

    def turn(value):
        return jnp.transpose(value.astype(F32))

    def turn_weights(u):
        turned = turn(w_in_ref[u]).astype(BF16)
        for i, block in enumerate((0, 2, 1, 3)):
            wt[u, i * H:(i + 1) * H] = turned[block * H:(block + 1) * H]

    def turn_small(u):
        wg[u] = turn(w_gate_ref[u]).astype(BF16)
        wo[u] = turn(w_out_ref[u]).astype(BF16)

    def column(ref, u, which, n):
        return jnp.transpose(jnp.broadcast_to(ref[u, which:which + 1, :n], (128, n)))

    def norm(values, gain, shift):
        center = jnp.mean(values, axis=0, keepdims=True)
        centred = values - center
        variance = jnp.mean(centred * centred, axis=0, keepdims=True)
        return (centred * lax.rsqrt(variance + EPS) * gain + shift).astype(BF16)

    def project(u, side, normed, mask, at, stride):
        both = dot(wt[u, side * 2 * H:(side + 1) * 2 * H, :], normed)
        value = both[:H] * (sigmoid(both[H:]) * mask)
        for t in range(q):
            lay[pl.ds(at + t, H, stride=stride), :] = value[:, t * 128:(t + 1) * 128]

    def pack(target, rows):
        hs = min(16, H)

        def some(g, carry):
            part = lay[pl.ds(g * hs * rows, hs * rows), :].astype(BF16)
            target[pl.ds(g * hs, hs)] = part.reshape(hs, rows, 128)
            return carry

        for_each(H // hs, some)

    def for_each(n, step):
        if n:
            lax.fori_loop(0, n, step, 0)

    def gates(u):
        def chunk(g, carry):
            gate[g] = sigmoid(dot(wg[u], nb[g]))
            return carry

        for_each(T // q, chunk)

    def put(source, target, s_sem, r_sem, some):
        for s in some:
            if s == here:
                pltpu.make_async_copy(source.at[me], target.at[me], r_sem).start()
            else:
                r, c = peer(s)
                pltpu.make_async_remote_copy(
                    src_ref=source.at[r * nc + c], dst_ref=target.at[me], send_sem=s_sem, recv_sem=r_sem,
                    device_id=(r, c), device_id_type=MESH,
                ).start()

    def put_block(i):
        put(send.at[i], got.at[i], send_sem.at[i], got_sem.at[i], shifts + [here])

    def put_left(half):
        put(send_left.at[half], got_left.at[half], left_send_sem.at[half], left_sem.at[half], shifts + [here])

    def put_back(u, half, some):
        put(prod.at[u, half], back.at[u, half], back_send_sem.at[u, half], back_sem.at[u, half], some)

    def arrive(target, r_sem):
        pltpu.make_async_copy(target, target, r_sem).wait()

    def sent(source, s_sem):
        part = source.at[pl.ds(0, H - 1)]
        pltpu.make_async_copy(part, part, s_sem).wait()

    def halves(tile):
        turned = pltpu.roll(tile, HALF, 1)
        zero = jnp.zeros_like(tile)
        return (
            (jnp.where(low, tile, zero).astype(BF16), jnp.where(low, turned, zero).astype(BF16)),
            (jnp.where(low, zero, turned).astype(BF16), jnp.where(low, zero, tile).astype(BF16)),
        )

    def build_outgoing():
        box = got.at[0]

        def step(r, carry):
            for c in range(nc):
                parts = halves(box[r * nc + c].astype(F32))
                for ip in range(2):
                    for p in range(2):
                        at = (r // 2) * 128 + ip * HALF + (r % 2) * 32 + p * T
                        big[pl.ds(pl.multiple_of(at, T), T), c * 128:(c + 1) * 128] = parts[ip][p]
            return carry

        for_each(nr, step)

    def line_up_outgoing(half):
        box = got_left.at[half]
        for c in range(nc):
            for r in range(0, nr, 2):
                pair = jnp.concatenate([box[r * nc + c].astype(F32), box[(r + 1) * nc + c].astype(F32)], axis=0)
                at = half * nr * B + r * B
                lhs[at:at + T, c * 128:(c + 1) * 128] = pair.astype(BF16)

    def build_incoming(half):
        box = got.at[1 + half]

        def step(g, carry):
            r = g * 2
            for c in range(nc):
                tile = jnp.concatenate(
                    [box[r * nc + c].astype(F32)[:B], box[(r + 1) * nc + c].astype(F32)[:B]], axis=0
                )
                parts = halves(tile)
                for ip in range(2):
                    for p in range(2):
                        at = ((ip * 2 + p) * 2 + half) * nr * B + g * T
                        big[pl.ds(pl.multiple_of(at, T), T), c * 128:(c + 1) * 128] = parts[ip][p]
            return carry

        for_each(nr // 2, step)

    def line_up_incoming(half):
        box = got.at[1 + half]
        for c in range(nc):
            block = jnp.concatenate([box[r * nc + c].astype(F32)[B:] for r in range(nr)], axis=0)
            turned = jnp.transpose(block).astype(BF16)
            for kp, hi, ip in itertools.product(range(2), range(2), range(2)):
                src = ((kp * 2 + hi) * 2 + ip) * T
                dst = (c * 2 + hi) * T
                at = ((ip * 2 + kp) * 2 + half) * nr * B
                lhs[dst:dst + T, at:at + nr * B] = turned[src:src + T, :]

    columns = sorted(range(Y), key=lambda d: -hops(d, Y))

    def contract_outgoing(half):
        for dy in columns:
            c0 = ys[dy] * 2
            span = pl.ds(pl.multiple_of(c0 * 128, 256), 256)
            value = dot(lhs[half * nr * B:(half + 1) * nr * B, :], big[span, :], NT)
            for c in range(2):
                part = value[:, c * 128:(c + 1) * 128].astype(BF16).reshape(nr, B, 128)
                for r in range(nr):
                    prod[0, half, r * nc + c0 + c] = part[r]
            put_back(0, half, [s for s in shifts + [here] if s[1] == dy])

    def contract_incoming():
        for dy in columns:
            c0 = ys[dy] * 2
            span = pl.ds(pl.multiple_of(c0 * 128, 256), 256)
            value = dot(lhs[...], big[:, span])
            for c in range(2):
                part = value[:, c * 128:(c + 1) * 128].astype(BF16).reshape(nr, 2, B, 128)
                for r in range(nr):
                    for half in range(2):
                        prod[1, half, r * nc + c0 + c] = part[r, half]
            put_back(1, 0, [s for s in shifts + [here] if s[1] == dy])
        put_back(1, 1, shifts + [here])

    def widen(u, half):
        hs = min(16, H)
        box = back.at[u, half]
        arrive(box, back_sem.at[u, half])

        def some(g, carry):
            lay2[pl.ds(g * hs * B, hs * B), :] = box[pl.ds(g * hs, hs)].astype(F32).reshape(hs * B, 128)
            return carry

        for_each(H // hs, some)

    def finish(u, half, row, factors):
        gain, shift = factors
        i2 = half * B + row
        normed = [norm(lay2[pl.ds(row + t, H, stride=B), :], gain, shift) for t in range(q)]
        update = dot(wo[u], jnp.concatenate(normed, axis=1))
        old = jnp.concatenate([held[i2 + t].astype(F32) for t in range(q)], axis=1)
        return old + gate[i2 // q] * update * flags(valid_s, valid_cols, i2)

    def from_pair(i2, n):
        top = pair_ref[pl.ds(i2, n)]
        bottom = pair_ref[pl.ds(i2 + T, n)]
        return jnp.concatenate([top, bottom], axis=1).reshape(n * 128, C)

    for copy in loads[:6]:
        copy.wait()
    turn_weights(0)
    pad_cols = col_flags(pad_v)
    gain, shift = column(gain_ref, 0, 0, C), column(shift_ref, 0, 0, C)

    def right_first(g, carry):
        i2 = g * q
        values = turn(from_pair(i2, q))
        normed = []
        for t in range(q):
            tile = values[:, t * 128:(t + 1) * 128]
            held[i2 + t] = tile.astype(BF16)
            normed.append(norm(tile, gain, shift))
        normed = jnp.concatenate(normed, axis=1)
        nb[g] = normed
        project(0, 1, normed, flags(pad_s, pad_cols, i2), i2, T)
        return carry

    for_each(T // q, right_first)
    pack(send.at[0], T)
    pl.semaphore_wait(barrier, H - 1)
    put_block(0)
    for half in range(2):
        def left_next(g, carry, half=half):
            i2 = half * B + g * q
            project(0, 0, nb[half * (B // q) + g], flags(pad_s, pad_cols, i2), g * q, B)
            return carry

        for_each(B // q, left_next)
        pack(send_left.at[half], B)
        put_left(half)
    for copy in loads[6:]:
        copy.wait()
    valid_cols = col_flags(valid_v)
    turn_small(0)
    gates(0)
    turn_weights(1)
    turn_small(1)
    factors = column(gain_ref, 0, 1, H), column(shift_ref, 0, 1, H)
    gain1, shift1 = column(gain_ref, 1, 0, C), column(shift_ref, 1, 0, C)
    arrive(got.at[0], got_sem.at[0])
    build_outgoing()
    for half in range(2):
        arrive(got_left.at[half], left_sem.at[half])
        line_up_outgoing(half)
        contract_outgoing(half)

    for half in range(2):
        widen(0, half)

        def middle(g, carry, half=half):
            i2 = half * B + g * q
            values = finish(0, half, g * q, factors).astype(BF16)
            normed = []
            for t in range(q):
                tile = values[:, t * 128:(t + 1) * 128]
                held[i2 + t] = tile
                normed.append(norm(tile.astype(F32), gain1, shift1))
            normed = jnp.concatenate(normed, axis=1)
            nb[half * (B // q) + g] = normed
            mask = flags(pad_s, pad_cols, i2)
            project(1, 1, normed, mask, g * q, T)
            project(1, 0, normed, mask, B + g * q, T)
            return carry

        for_each(B // q, middle)
        pack(send.at[1 + half], T)
        put_block(1 + half)
    gates(1)
    factors = column(gain_ref, 1, 1, H), column(shift_ref, 1, 1, H)
    for half in range(2):
        arrive(got.at[1 + half], got_sem.at[1 + half])
        build_incoming(half)
        line_up_incoming(half)
    contract_incoming()
    outs = []
    for half in range(2):
        widen(1, half)

        def end(g, carry, half=half):
            values = finish(1, half, g * q, factors)
            for t in range(q):
                i2 = half * B + g * q + t
                value = jnp.transpose(values[:, t * 128:(t + 1) * 128]).astype(BF16)
                out_ref[i2] = value[:HALF]
                out_ref[i2 + T] = value[HALF:]
            return carry

        for_each(B // q, end)
        for i, at in enumerate((half * B, T + half * B)):
            rows = pl.ds(at, B)
            copy = pltpu.make_async_copy(out_ref.at[rows], out_hbm.at[rows], out_sem.at[half * 2 + i])
            copy.start()
            outs.append(copy)
    for i in range(3):
        sent(send.at[i], send_sem.at[i])
    for half in range(2):
        sent(send_left.at[half], left_send_sem.at[half])
        for u in range(2):
            sent(prod.at[u, half], back_send_sem.at[u, half])
    for copy in outs:
        copy.wait()


def solution(mesh):
    nr, nc = mesh.shape["row"], mesh.shape["col"]

    def local(pair, pad_mask, valid_flags, w_in, w_gate, w_out, gains, shifts):
        H = nr * nc
        C = pair.shape[-1]
        hbm = pl.BlockSpec(memory_space=pl.ANY)
        pad_mask = pad_mask.reshape(-1, 128)
        valid_flags = valid_flags.reshape(-1, 128)
        operands = (pair, pad_mask, valid_flags, w_in, w_gate, w_out, gains, shifts)
        dma = pltpu.SemaphoreType.DMA
        return pl.pallas_call(
            functools.partial(kernel, nr, nc),
            out_shape=jax.ShapeDtypeStruct(pair.shape, BF16),
            in_specs=[hbm] * len(operands),
            out_specs=hbm,
            scratch_shapes=[pltpu.VMEM(a.shape, a.dtype) for a in operands] + [
                pltpu.SMEM(pad_mask.shape, pad_mask.dtype),
                pltpu.SMEM(valid_flags.shape, valid_flags.dtype),
                pltpu.VMEM(pair.shape, BF16),
                pltpu.VMEM((3, H, T, 128), BF16),
                pltpu.VMEM((3, H, T, 128), BF16),
                pltpu.VMEM((2, H, T // 2, 128), BF16),
                pltpu.VMEM((2, H, T // 2, 128), BF16),
                pltpu.VMEM((2, 2, H, T // 2, 128), BF16),
                pltpu.VMEM((2, 2, H, T // 2, 128), BF16),
                pltpu.VMEM((2, 4 * H, C), BF16),
                pltpu.VMEM((2, C, C), BF16),
                pltpu.VMEM((2, C, H), BF16),
                pltpu.VMEM((T // 4, C, 512), BF16),
                pltpu.VMEM((T // 4, C, 512), F32),
                pltpu.VMEM((T, C, 128), BF16),
                pltpu.VMEM((H * T, 128), F32),
                pltpu.VMEM((H * T // 2, 128), F32),
                pltpu.VMEM((nc * 128, nc * 128), BF16),
                pltpu.VMEM((nr * T, nc * 128), BF16),
                dma((10,)), dma((3,)), dma((3,)), dma((2,)), dma((2,)), dma((2, 2)), dma((2, 2)), dma((4,)),
            ],
            compiler_params=pltpu.CompilerParams(
                collective_id=0, has_side_effects=True, vmem_limit_bytes=60 * 1024 * 1024
            ),
        )(*operands)

    placed = (P("row", "col", None), P(), P(), P(), P(), P(), P(), P())
    return jax.shard_map(
        local, mesh=mesh, in_specs=placed, out_specs=P("row", "col", None), check_vma=False
    )
```

```python
import functools
import itertools

import jax
import jax.numpy as jnp
from jax import lax
from jax.experimental import pallas as pl
from jax.experimental.pallas import tpu as pltpu
from jax.sharding import PartitionSpec as P

EPS = 1e-05
MESH = pl.DeviceIdType.MESH
F32 = jnp.float32
BF16 = jnp.bfloat16
T = 16
HALF = 64
NN = (((1,), (0,)), ((), ()))
NT = (((1,), (1,)), ((), ()))


def sigmoid(v):
    return 0.5 * jnp.tanh(0.5 * v) + 0.5


def dot(a, b, dims=NN):
    return lax.dot_general(a, b, dims, preferred_element_type=F32)


def hops(shift, size):
    return min(shift, size - shift)


def kernel(
    nr, nc, pair_hbm, pad_hbm, valid_hbm, w_in_hbm, w_gate_hbm, w_out_hbm, gain_hbm, shift_hbm,
    out_hbm,
    pair_ref, pad_v, valid_v, w_in_ref, w_gate_ref, w_out_ref, gain_ref, shift_ref, pad_s, valid_s, out_ref,
    send, got, send_left, got_left, prod, back, wt, wg, wo, nb, gate, held, lay, lay2, big, lhs,
    load_sem, send_sem, got_sem, left_send_sem, left_sem, back_send_sem, back_sem, out_sem,
):
    H = nr * nc
    C = pair_ref.shape[-1]
    X, Y = nr // 4, nc // 2
    my_r = lax.axis_index("row")
    my_c = lax.axis_index("col")
    me = my_r * nc + my_c

    xs = [(my_r // 4 + d) % X for d in range(X)]
    ys = [(my_c // 2 + d) % Y for d in range(Y)]
    zs = [((my_c % 2) * 2 + (my_r // 2) % 2 + d) % 4 for d in range(4)]
    ks = [(my_r % 2 + d) % 2 for d in range(2)]
    row_parts = [[xs[dx] * 4 + ks[dk] for dk in range(2)] for dx in range(X)]
    z_lo = [(z % 2) * 2 for z in zs]
    z_hi = [z // 2 for z in zs]

    def peer(shift):
        dx, dy, dz, dk = shift
        return row_parts[dx][dk] + z_lo[dz], ys[dy] * 2 + z_hi[dz]

    def distance(shift):
        dx, dy, dz, dk = shift
        return hops(dx, X) + hops(dy, Y) + hops(dz, 4) + 0.3 * dk

    here = (0, 0, 0, 0)
    shifts = [s for s in itertools.product(range(X), range(Y), range(4), range(2)) if s != here]
    shifts.sort(key=lambda s: (-distance(s), (s[0] * 37 + s[1] * 53 + s[2] * 71 + s[3] * 19) % 29))

    loads = []
    for i, (a, b) in enumerate((
        (pair_hbm, pair_ref), (w_in_hbm, w_in_ref), (gain_hbm, gain_ref), (shift_hbm, shift_ref), (pad_hbm, pad_v),
        (pad_hbm, pad_s), (w_gate_hbm, w_gate_ref), (w_out_hbm, w_out_ref), (valid_hbm, valid_v),
        (valid_hbm, valid_s),
    )):
        copy = pltpu.make_async_copy(a, b, load_sem.at[i])
        copy.start()
        loads.append(copy)

    barrier = pltpu.get_barrier_semaphore()
    for s in shifts:
        pl.semaphore_signal(barrier, inc=1, device_id=peer(s), device_id_type=MESH)

    lane = lax.broadcasted_iota(jnp.int32, (1, 128), 1)
    low = lane < HALF
    odd = my_c % 2

    def col_flags(ref):
        row = ref[pl.ds(my_c // 2, 1), :].astype(F32)
        turned = pltpu.roll(row, HALF, 1)
        lo = jnp.where(odd == 1, turned, row)
        hi = jnp.where(odd == 1, row, turned)
        return jnp.where(low, lo, hi)

    def flag(ref, i):
        return ref[i // 128, i % 128].astype(F32)

    q = 4
    B = T // 2

    def flags(ref, cols, i2):
        tiles = []
        for t in range(q):
            top = flag(ref, my_r * 32 + i2 + t)
            bottom = flag(ref, my_r * 32 + T + i2 + t)
            tiles.append(jnp.where(low, top, bottom) * cols)
        return jnp.concatenate(tiles, axis=1)

    def turn(value):
        return jnp.transpose(value.astype(F32))

    def turn_weights(u):
        turned = turn(w_in_ref[u]).astype(BF16)
        for i, block in enumerate((0, 2, 1, 3)):
            wt[u, i * H:(i + 1) * H] = turned[block * H:(block + 1) * H]

    def turn_small(u):
        wg[u] = turn(w_gate_ref[u]).astype(BF16)
        wo[u] = turn(w_out_ref[u]).astype(BF16)

    def column(ref, u, which, n):
        return jnp.transpose(jnp.broadcast_to(ref[u, which:which + 1, :n], (128, n)))

    def norm(values, gain, shift):
        center = jnp.mean(values, axis=0, keepdims=True)
        centred = values - center
        variance = jnp.mean(centred * centred, axis=0, keepdims=True)
        return (centred * lax.rsqrt(variance + EPS) * gain + shift).astype(BF16)

    def project(u, side, normed, mask, at, stride):
        both = dot(wt[u, side * 2 * H:(side + 1) * 2 * H, :], normed)
        value = both[:H] * (sigmoid(both[H:]) * mask)
        for t in range(q):
            lay[pl.ds(at + t, H, stride=stride), :] = value[:, t * 128:(t + 1) * 128]

    def pack(target, rows):
        hs = min(16, H)

        def some(g, carry):
            part = lay[pl.ds(g * hs * rows, hs * rows), :].astype(BF16)
            target[pl.ds(g * hs, hs)] = part.reshape(hs, rows, 128)
            return carry

        for_each(H // hs, some)

    def for_each(n, step):
        if n:
            lax.fori_loop(0, n, step, 0)

    def gates(u):
        def chunk(g, carry):
            gate[g] = sigmoid(dot(wg[u], nb[g]))
            return carry

        for_each(T // q, chunk)

    def put(source, target, s_sem, r_sem, some):
        for s in some:
            if s == here:
                pltpu.make_async_copy(source.at[me], target.at[me], r_sem).start()
            else:
                r, c = peer(s)
                pltpu.make_async_remote_copy(
                    src_ref=source.at[r * nc + c], dst_ref=target.at[me], send_sem=s_sem, recv_sem=r_sem,
                    device_id=(r, c), device_id_type=MESH,
                ).start()

    def put_block(i):
        put(send.at[i], got.at[i], send_sem.at[i], got_sem.at[i], shifts + [here])

    def put_left(half):
        put(send_left.at[half], got_left.at[half], left_send_sem.at[half], left_sem.at[half], shifts + [here])

    def put_back(u, half, some):
        put(prod.at[u, half], back.at[u, half], back_send_sem.at[u, half], back_sem.at[u, half], some)

    def arrive(target, r_sem):
        pltpu.make_async_copy(target, target, r_sem).wait()

    def sent(source, s_sem):
        part = source.at[pl.ds(0, H - 1)]
        pltpu.make_async_copy(part, part, s_sem).wait()

    def halves(tile):
        turned = pltpu.roll(tile, HALF, 1)
        zero = jnp.zeros_like(tile)
        return (
            (jnp.where(low, tile, zero).astype(BF16), jnp.where(low, turned, zero).astype(BF16)),
            (jnp.where(low, zero, turned).astype(BF16), jnp.where(low, zero, tile).astype(BF16)),
        )

    def build_outgoing():
        box = got.at[0]

        def step(r, carry):
            for c in range(nc):
                parts = halves(box[r * nc + c].astype(F32))
                for ip in range(2):
                    for p in range(2):
                        at = (r // 2) * 128 + ip * HALF + (r % 2) * 32 + p * T
                        big[pl.ds(pl.multiple_of(at, T), T), c * 128:(c + 1) * 128] = parts[ip][p]
            return carry

        for_each(nr, step)

    def line_up_outgoing(half):
        box = got_left.at[half]
        for c in range(nc):
            for r in range(0, nr, 2):
                pair = jnp.concatenate([box[r * nc + c].astype(F32), box[(r + 1) * nc + c].astype(F32)], axis=0)
                at = half * nr * B + r * B
                lhs[at:at + T, c * 128:(c + 1) * 128] = pair.astype(BF16)

    def build_incoming(half):
        box = got.at[1 + half]

        def step(g, carry):
            r = g * 2
            for c in range(nc):
                tile = jnp.concatenate(
                    [box[r * nc + c].astype(F32)[:B], box[(r + 1) * nc + c].astype(F32)[:B]], axis=0
                )
                parts = halves(tile)
                for ip in range(2):
                    for p in range(2):
                        at = ((ip * 2 + p) * 2 + half) * nr * B + g * T
                        big[pl.ds(pl.multiple_of(at, T), T), c * 128:(c + 1) * 128] = parts[ip][p]
            return carry

        for_each(nr // 2, step)

    def line_up_incoming(half):
        box = got.at[1 + half]
        for c in range(nc):
            block = jnp.concatenate([box[r * nc + c].astype(F32)[B:] for r in range(nr)], axis=0)
            turned = jnp.transpose(block).astype(BF16)
            for kp, hi, ip in itertools.product(range(2), range(2), range(2)):
                src = ((kp * 2 + hi) * 2 + ip) * T
                dst = (c * 2 + hi) * T
                at = ((ip * 2 + kp) * 2 + half) * nr * B
                lhs[dst:dst + T, at:at + nr * B] = turned[src:src + T, :]

    columns = sorted(range(Y), key=lambda d: -hops(d, Y))

    def contract_outgoing(half):
        for dy in columns:
            c0 = ys[dy] * 2
            span = pl.ds(pl.multiple_of(c0 * 128, 256), 256)
            value = dot(lhs[half * nr * B:(half + 1) * nr * B, :], big[span, :], NT)
            for c in range(2):
                part = value[:, c * 128:(c + 1) * 128].astype(BF16).reshape(nr, B, 128)
                for r in range(nr):
                    prod[0, half, r * nc + c0 + c] = part[r]
        put_back(0, half, shifts + [here])

    def contract_incoming():
        for dy in columns:
            c0 = ys[dy] * 2
            span = pl.ds(pl.multiple_of(c0 * 128, 256), 256)
            value = dot(lhs[...], big[:, span])
            for c in range(2):
                part = value[:, c * 128:(c + 1) * 128].astype(BF16).reshape(nr, 2, B, 128)
                for r in range(nr):
                    for half in range(2):
                        prod[1, half, r * nc + c0 + c] = part[r, half]
        put_back(1, 0, shifts + [here])
        put_back(1, 1, shifts + [here])

    def widen(u, half):
        hs = min(16, H)
        box = back.at[u, half]
        arrive(box, back_sem.at[u, half])

        def some(g, carry):
            lay2[pl.ds(g * hs * B, hs * B), :] = box[pl.ds(g * hs, hs)].astype(F32).reshape(hs * B, 128)
            return carry

        for_each(H // hs, some)

    def finish(u, half, row, factors):
        gain, shift = factors
        i2 = half * B + row
        normed = [norm(lay2[pl.ds(row + t, H, stride=B), :], gain, shift) for t in range(q)]
        update = dot(wo[u], jnp.concatenate(normed, axis=1))
        old = jnp.concatenate([held[i2 + t].astype(F32) for t in range(q)], axis=1)
        return old + gate[i2 // q] * update * flags(valid_s, valid_cols, i2)

    def from_pair(i2, n):
        top = pair_ref[pl.ds(i2, n)]
        bottom = pair_ref[pl.ds(i2 + T, n)]
        return jnp.concatenate([top, bottom], axis=1).reshape(n * 128, C)

    for copy in loads[:6]:
        copy.wait()
    turn_weights(0)
    pad_cols = col_flags(pad_v)
    gain, shift = column(gain_ref, 0, 0, C), column(shift_ref, 0, 0, C)

    def right_first(g, carry):
        i2 = g * q
        values = turn(from_pair(i2, q))
        normed = []
        for t in range(q):
            tile = values[:, t * 128:(t + 1) * 128]
            held[i2 + t] = tile.astype(BF16)
            normed.append(norm(tile, gain, shift))
        normed = jnp.concatenate(normed, axis=1)
        nb[g] = normed
        project(0, 1, normed, flags(pad_s, pad_cols, i2), i2, T)
        return carry

    for_each(T // q, right_first)
    pack(send.at[0], T)
    pl.semaphore_wait(barrier, H - 1)
    put_block(0)
    for half in range(2):
        def left_next(g, carry, half=half):
            i2 = half * B + g * q
            project(0, 0, nb[half * (B // q) + g], flags(pad_s, pad_cols, i2), g * q, B)
            return carry

        for_each(B // q, left_next)
        pack(send_left.at[half], B)
        if half == 0:
            sent(send.at[0], send_sem.at[0])
        else:
            sent(send_left.at[0], left_send_sem.at[0])
        put_left(half)
    for copy in loads[6:]:
        copy.wait()
    valid_cols = col_flags(valid_v)
    turn_small(0)
    gates(0)
    turn_weights(1)
    turn_small(1)
    factors = column(gain_ref, 0, 1, H), column(shift_ref, 0, 1, H)
    gain1, shift1 = column(gain_ref, 1, 0, C), column(shift_ref, 1, 0, C)
    arrive(got.at[0], got_sem.at[0])
    build_outgoing()
    for half in range(2):
        arrive(got_left.at[half], left_sem.at[half])
        line_up_outgoing(half)
        contract_outgoing(half)

    for half in range(2):
        widen(0, half)

        def middle(g, carry, half=half):
            i2 = half * B + g * q
            values = finish(0, half, g * q, factors).astype(BF16)
            normed = []
            for t in range(q):
                tile = values[:, t * 128:(t + 1) * 128]
                held[i2 + t] = tile
                normed.append(norm(tile.astype(F32), gain1, shift1))
            normed = jnp.concatenate(normed, axis=1)
            nb[half * (B // q) + g] = normed
            mask = flags(pad_s, pad_cols, i2)
            project(1, 1, normed, mask, g * q, T)
            project(1, 0, normed, mask, B + g * q, T)
            return carry

        for_each(B // q, middle)
        pack(send.at[1 + half], T)
        put_block(1 + half)
    gates(1)
    factors = column(gain_ref, 1, 1, H), column(shift_ref, 1, 1, H)
    for half in range(2):
        arrive(got.at[1 + half], got_sem.at[1 + half])
        build_incoming(half)
        line_up_incoming(half)
    contract_incoming()
    outs = []
    for half in range(2):
        widen(1, half)

        def end(g, carry, half=half):
            values = finish(1, half, g * q, factors)
            for t in range(q):
                i2 = half * B + g * q + t
                value = jnp.transpose(values[:, t * 128:(t + 1) * 128]).astype(BF16)
                out_ref[i2] = value[:HALF]
                out_ref[i2 + T] = value[HALF:]
            return carry

        for_each(B // q, end)
        for i, at in enumerate((half * B, T + half * B)):
            rows = pl.ds(at, B)
            copy = pltpu.make_async_copy(out_ref.at[rows], out_hbm.at[rows], out_sem.at[half * 2 + i])
            copy.start()
            outs.append(copy)
    for i in (1, 2):
        sent(send.at[i], send_sem.at[i])
    sent(send_left.at[1], left_send_sem.at[1])
    for half in range(2):
        for u in range(2):
            sent(prod.at[u, half], back_send_sem.at[u, half])
    for copy in outs:
        copy.wait()


def solution(mesh):
    nr, nc = mesh.shape["row"], mesh.shape["col"]

    def local(pair, pad_mask, valid_flags, w_in, w_gate, w_out, gains, shifts):
        H = nr * nc
        C = pair.shape[-1]
        hbm = pl.BlockSpec(memory_space=pl.ANY)
        pad_mask = pad_mask.reshape(-1, 128)
        valid_flags = valid_flags.reshape(-1, 128)
        operands = (pair, pad_mask, valid_flags, w_in, w_gate, w_out, gains, shifts)
        dma = pltpu.SemaphoreType.DMA
        return pl.pallas_call(
            functools.partial(kernel, nr, nc),
            out_shape=jax.ShapeDtypeStruct(pair.shape, BF16),
            in_specs=[hbm] * len(operands),
            out_specs=hbm,
            scratch_shapes=[pltpu.VMEM(a.shape, a.dtype) for a in operands] + [
                pltpu.SMEM(pad_mask.shape, pad_mask.dtype),
                pltpu.SMEM(valid_flags.shape, valid_flags.dtype),
                pltpu.VMEM(pair.shape, BF16),
                pltpu.VMEM((3, H, T, 128), BF16),
                pltpu.VMEM((3, H, T, 128), BF16),
                pltpu.VMEM((2, H, T // 2, 128), BF16),
                pltpu.VMEM((2, H, T // 2, 128), BF16),
                pltpu.VMEM((2, 2, H, T // 2, 128), BF16),
                pltpu.VMEM((2, 2, H, T // 2, 128), BF16),
                pltpu.VMEM((2, 4 * H, C), BF16),
                pltpu.VMEM((2, C, C), BF16),
                pltpu.VMEM((2, C, H), BF16),
                pltpu.VMEM((T // 4, C, 512), BF16),
                pltpu.VMEM((T // 4, C, 512), F32),
                pltpu.VMEM((T, C, 128), BF16),
                pltpu.VMEM((H * T, 128), F32),
                pltpu.VMEM((H * T // 2, 128), F32),
                pltpu.VMEM((nc * 128, nc * 128), BF16),
                pltpu.VMEM((nr * T, nc * 128), BF16),
                dma((10,)), dma((3,)), dma((3,)), dma((2,)), dma((2,)), dma((2, 2)), dma((2, 2)), dma((4,)),
            ],
            compiler_params=pltpu.CompilerParams(
                collective_id=0, has_side_effects=True, vmem_limit_bytes=60 * 1024 * 1024
            ),
        )(*operands)

    placed = (P("row", "col", None), P(), P(), P(), P(), P(), P(), P())
    return jax.shard_map(
        local, mesh=mesh, in_specs=placed, out_specs=P("row", "col", None), check_vma=False
    )
```

```python
import functools
import itertools

import jax
import jax.numpy as jnp
from jax import lax
from jax.experimental import pallas as pl
from jax.experimental.pallas import tpu as pltpu
from jax.sharding import PartitionSpec as P

EPS = 1e-05
MESH = pl.DeviceIdType.MESH
F32 = jnp.float32
BF16 = jnp.bfloat16
T = 16
HALF = 64
NN = (((1,), (0,)), ((), ()))
NT = (((1,), (1,)), ((), ()))


def sigmoid(v):
    return 0.5 * jnp.tanh(0.5 * v) + 0.5


def dot(a, b, dims=NN):
    return lax.dot_general(a, b, dims, preferred_element_type=F32)


def hops(shift, size):
    return min(shift, size - shift)


def kernel(
    nr, nc, pair_hbm, pad_hbm, valid_hbm, w_in_hbm, w_gate_hbm, w_out_hbm, gain_hbm, shift_hbm,
    out_hbm,
    pair_ref, pad_v, valid_v, w_in_ref, w_gate_ref, w_out_ref, gain_ref, shift_ref, pad_s, valid_s, out_ref,
    send, got, send_left, got_left, prod, back, wt, wg, wo, nb, gate, held, lay, lay2, big, lhs,
    load_sem, send_sem, got_sem, left_send_sem, left_sem, back_send_sem, back_sem, out_sem,
):
    H = nr * nc
    C = pair_ref.shape[-1]
    X, Y = nr // 4, nc // 2
    my_r = lax.axis_index("row")
    my_c = lax.axis_index("col")
    me = my_r * nc + my_c

    xs = [(my_r // 4 + d) % X for d in range(X)]
    ys = [(my_c // 2 + d) % Y for d in range(Y)]
    zs = [((my_c % 2) * 2 + (my_r // 2) % 2 + d) % 4 for d in range(4)]
    ks = [(my_r % 2 + d) % 2 for d in range(2)]
    row_parts = [[xs[dx] * 4 + ks[dk] for dk in range(2)] for dx in range(X)]
    z_lo = [(z % 2) * 2 for z in zs]
    z_hi = [z // 2 for z in zs]

    def peer(shift):
        dx, dy, dz, dk = shift
        return row_parts[dx][dk] + z_lo[dz], ys[dy] * 2 + z_hi[dz]

    def distance(shift):
        dx, dy, dz, dk = shift
        return hops(dx, X) + hops(dy, Y) + hops(dz, 4) + 0.3 * dk

    here = (0, 0, 0, 0)
    shifts = [s for s in itertools.product(range(X), range(Y), range(4), range(2)) if s != here]
    shifts.sort(key=lambda s: (-distance(s), (s[0] * 37 + s[1] * 53 + s[2] * 71 + s[3] * 19) % 29))

    loads = []
    for i, (a, b) in enumerate((
        (pair_hbm, pair_ref), (w_in_hbm, w_in_ref), (gain_hbm, gain_ref), (shift_hbm, shift_ref), (pad_hbm, pad_v),
        (pad_hbm, pad_s), (w_gate_hbm, w_gate_ref), (w_out_hbm, w_out_ref), (valid_hbm, valid_v),
        (valid_hbm, valid_s),
    )):
        copy = pltpu.make_async_copy(a, b, load_sem.at[i])
        copy.start()
        loads.append(copy)

    barrier = pltpu.get_barrier_semaphore()
    for s in shifts:
        pl.semaphore_signal(barrier, inc=1, device_id=peer(s), device_id_type=MESH)

    lane = lax.broadcasted_iota(jnp.int32, (1, 128), 1)
    low = lane < HALF
    odd = my_c % 2

    def col_flags(ref):
        row = ref[pl.ds(my_c // 2, 1), :].astype(F32)
        turned = pltpu.roll(row, HALF, 1)
        lo = jnp.where(odd == 1, turned, row)
        hi = jnp.where(odd == 1, row, turned)
        return jnp.where(low, lo, hi)

    def flag(ref, i):
        return ref[i // 128, i % 128].astype(F32)

    q = 4
    B = T // 2

    def flags(ref, cols, i2):
        tiles = []
        for t in range(q):
            top = flag(ref, my_r * 32 + i2 + t)
            bottom = flag(ref, my_r * 32 + T + i2 + t)
            tiles.append(jnp.where(low, top, bottom) * cols)
        return jnp.concatenate(tiles, axis=1)

    def turn(value):
        return jnp.transpose(value.astype(F32))

    def turn_weights(u):
        turned = turn(w_in_ref[u]).astype(BF16)
        for i, block in enumerate((0, 2, 1, 3)):
            wt[u, i * H:(i + 1) * H] = turned[block * H:(block + 1) * H]

    def turn_small(u):
        wg[u] = turn(w_gate_ref[u]).astype(BF16)
        wo[u] = turn(w_out_ref[u]).astype(BF16)

    def column(ref, u, which, n):
        return jnp.transpose(jnp.broadcast_to(ref[u, which:which + 1, :n], (128, n)))

    def norm(values, gain, shift):
        center = jnp.mean(values, axis=0, keepdims=True)
        centred = values - center
        variance = jnp.mean(centred * centred, axis=0, keepdims=True)
        return (centred * lax.rsqrt(variance + EPS) * gain + shift).astype(BF16)

    def project(u, side, normed, mask, at, stride):
        both = dot(wt[u, side * 2 * H:(side + 1) * 2 * H, :], normed)
        value = both[:H] * (sigmoid(both[H:]) * mask)
        for t in range(q):
            lay[pl.ds(at + t, H, stride=stride), :] = value[:, t * 128:(t + 1) * 128]

    def pack(target, rows):
        hs = min(16, H)

        def some(g, carry):
            part = lay[pl.ds(g * hs * rows, hs * rows), :].astype(BF16)
            target[pl.ds(g * hs, hs)] = part.reshape(hs, rows, 128)
            return carry

        for_each(H // hs, some)

    def for_each(n, step):
        if n:
            lax.fori_loop(0, n, step, 0)

    def gates(u):
        def chunk(g, carry):
            gate[g] = sigmoid(dot(wg[u], nb[g]))
            return carry

        for_each(T // q, chunk)

    def put(source, target, s_sem, r_sem, some):
        for s in some:
            if s == here:
                pltpu.make_async_copy(source.at[me], target.at[me], r_sem).start()
            else:
                r, c = peer(s)
                pltpu.make_async_remote_copy(
                    src_ref=source.at[r * nc + c], dst_ref=target.at[me], send_sem=s_sem, recv_sem=r_sem,
                    device_id=(r, c), device_id_type=MESH,
                ).start()

    def put_block(i):
        put(send.at[i], got.at[i], send_sem.at[i], got_sem.at[i], shifts + [here])

    def put_left(half):
        put(send_left.at[half], got_left.at[half], left_send_sem.at[half], left_sem.at[half], shifts + [here])

    def put_back(u, half, some):
        put(prod.at[u, half], back.at[u, half], back_send_sem.at[u, half], back_sem.at[u, half], some)

    def arrive(target, r_sem):
        pltpu.make_async_copy(target, target, r_sem).wait()

    def sent(source, s_sem):
        part = source.at[pl.ds(0, H - 1)]
        pltpu.make_async_copy(part, part, s_sem).wait()

    def halves(tile):
        turned = pltpu.roll(tile, HALF, 1)
        zero = jnp.zeros_like(tile)
        return (
            (jnp.where(low, tile, zero).astype(BF16), jnp.where(low, turned, zero).astype(BF16)),
            (jnp.where(low, zero, turned).astype(BF16), jnp.where(low, zero, tile).astype(BF16)),
        )

    def build_outgoing():
        box = got.at[0]

        def step(r, carry):
            for c in range(nc):
                parts = halves(box[r * nc + c].astype(F32))
                for ip in range(2):
                    for p in range(2):
                        at = (r // 2) * 128 + ip * HALF + (r % 2) * 32 + p * T
                        big[pl.ds(pl.multiple_of(at, T), T), c * 128:(c + 1) * 128] = parts[ip][p]
            return carry

        for_each(nr, step)

    def line_up_outgoing(half):
        box = got_left.at[half]
        for c in range(nc):
            for r in range(0, nr, 2):
                pair = jnp.concatenate([box[r * nc + c].astype(F32), box[(r + 1) * nc + c].astype(F32)], axis=0)
                at = half * nr * B + r * B
                lhs[at:at + T, c * 128:(c + 1) * 128] = pair.astype(BF16)

    def build_incoming(half):
        box = got.at[1 + half]

        def step(g, carry):
            r = g * 2
            for c in range(nc):
                tile = jnp.concatenate(
                    [box[r * nc + c].astype(F32)[:B], box[(r + 1) * nc + c].astype(F32)[:B]], axis=0
                )
                parts = halves(tile)
                for ip in range(2):
                    for p in range(2):
                        at = ((ip * 2 + p) * 2 + half) * nr * B + g * T
                        big[pl.ds(pl.multiple_of(at, T), T), c * 128:(c + 1) * 128] = parts[ip][p]
            return carry

        for_each(nr // 2, step)

    def line_up_incoming(half):
        box = got.at[1 + half]
        for c in range(nc):
            block = jnp.concatenate([box[r * nc + c].astype(F32)[B:] for r in range(nr)], axis=0)
            turned = jnp.transpose(block).astype(BF16)
            for kp, hi, ip in itertools.product(range(2), range(2), range(2)):
                src = ((kp * 2 + hi) * 2 + ip) * T
                dst = (c * 2 + hi) * T
                at = ((ip * 2 + kp) * 2 + half) * nr * B
                lhs[dst:dst + T, at:at + nr * B] = turned[src:src + T, :]

    columns = sorted(range(Y), key=lambda d: -hops(d, Y))

    def contract_outgoing(half):
        for dy in columns:
            c0 = ys[dy] * 2
            span = pl.ds(pl.multiple_of(c0 * 128, 256), 256)
            value = dot(lhs[half * nr * B:(half + 1) * nr * B, :], big[span, :], NT)
            for c in range(2):
                part = value[:, c * 128:(c + 1) * 128].astype(BF16).reshape(nr, B, 128)
                for r in range(nr):
                    prod[0, half, r * nc + c0 + c] = part[r]
        put_back(0, half, shifts + [here])

    def contract_incoming():
        for dy in columns:
            c0 = ys[dy] * 2
            span = pl.ds(pl.multiple_of(c0 * 128, 256), 256)
            value = dot(lhs[...], big[:, span])
            for c in range(2):
                part = value[:, c * 128:(c + 1) * 128].astype(BF16).reshape(nr, 2, B, 128)
                for r in range(nr):
                    for half in range(2):
                        prod[1, half, r * nc + c0 + c] = part[r, half]
        put_back(1, 0, shifts + [here])
        put_back(1, 1, shifts + [here])

    def widen(u, half):
        hs = min(16, H)
        box = back.at[u, half]
        arrive(box, back_sem.at[u, half])

        def some(g, carry):
            lay2[pl.ds(g * hs * B, hs * B), :] = box[pl.ds(g * hs, hs)].astype(F32).reshape(hs * B, 128)
            return carry

        for_each(H // hs, some)

    def finish(u, half, row, factors):
        gain, shift = factors
        i2 = half * B + row
        normed = [norm(lay2[pl.ds(row + t, H, stride=B), :], gain, shift) for t in range(q)]
        update = dot(wo[u], jnp.concatenate(normed, axis=1))
        old = jnp.concatenate([held[i2 + t].astype(F32) for t in range(q)], axis=1)
        return old + gate[i2 // q] * update * flags(valid_s, valid_cols, i2)

    def from_pair(i2, n):
        top = pair_ref[pl.ds(i2, n)]
        bottom = pair_ref[pl.ds(i2 + T, n)]
        return jnp.concatenate([top, bottom], axis=1).reshape(n * 128, C)

    for copy in loads[:6]:
        copy.wait()
    turn_weights(0)
    pad_cols = col_flags(pad_v)
    gain, shift = column(gain_ref, 0, 0, C), column(shift_ref, 0, 0, C)

    def right_first(g, carry):
        i2 = g * q
        values = turn(from_pair(i2, q))
        normed = []
        for t in range(q):
            tile = values[:, t * 128:(t + 1) * 128]
            held[i2 + t] = tile.astype(BF16)
            normed.append(norm(tile, gain, shift))
        normed = jnp.concatenate(normed, axis=1)
        nb[g] = normed
        project(0, 1, normed, flags(pad_s, pad_cols, i2), i2, T)
        return carry

    for_each(T // q, right_first)
    pack(send.at[0], T)
    pl.semaphore_wait(barrier, H - 1)
    put_block(0)
    for half in range(2):
        def left_next(g, carry, half=half):
            i2 = half * B + g * q
            project(0, 0, nb[half * (B // q) + g], flags(pad_s, pad_cols, i2), g * q, B)
            return carry

        for_each(B // q, left_next)
        pack(send_left.at[half], B)
        if half == 0:
            for copy in loads[6:]:
                copy.wait()
            turn_small(0)
            gates(0)
            sent(send.at[0], send_sem.at[0])
        else:
            turn_weights(1)
            turn_small(1)
            sent(send_left.at[0], left_send_sem.at[0])
        put_left(half)
    valid_cols = col_flags(valid_v)
    factors = column(gain_ref, 0, 1, H), column(shift_ref, 0, 1, H)
    gain1, shift1 = column(gain_ref, 1, 0, C), column(shift_ref, 1, 0, C)
    arrive(got.at[0], got_sem.at[0])
    build_outgoing()
    for half in range(2):
        arrive(got_left.at[half], left_sem.at[half])
        line_up_outgoing(half)
        contract_outgoing(half)

    for half in range(2):
        widen(0, half)

        def middle(g, carry, half=half):
            i2 = half * B + g * q
            values = finish(0, half, g * q, factors).astype(BF16)
            normed = []
            for t in range(q):
                tile = values[:, t * 128:(t + 1) * 128]
                held[i2 + t] = tile
                normed.append(norm(tile.astype(F32), gain1, shift1))
            normed = jnp.concatenate(normed, axis=1)
            nb[half * (B // q) + g] = normed
            mask = flags(pad_s, pad_cols, i2)
            project(1, 1, normed, mask, g * q, T)
            project(1, 0, normed, mask, B + g * q, T)
            return carry

        for_each(B // q, middle)
        pack(send.at[1 + half], T)
        put_block(1 + half)
    gates(1)
    factors = column(gain_ref, 1, 1, H), column(shift_ref, 1, 1, H)
    for half in range(2):
        arrive(got.at[1 + half], got_sem.at[1 + half])
        build_incoming(half)
        line_up_incoming(half)
    contract_incoming()
    outs = []
    for half in range(2):
        widen(1, half)

        def end(g, carry, half=half):
            values = finish(1, half, g * q, factors)
            for t in range(q):
                i2 = half * B + g * q + t
                value = jnp.transpose(values[:, t * 128:(t + 1) * 128]).astype(BF16)
                out_ref[i2] = value[:HALF]
                out_ref[i2 + T] = value[HALF:]
            return carry

        for_each(B // q, end)
        for i, at in enumerate((half * B, T + half * B)):
            rows = pl.ds(at, B)
            copy = pltpu.make_async_copy(out_ref.at[rows], out_hbm.at[rows], out_sem.at[half * 2 + i])
            copy.start()
            outs.append(copy)
    for i in (1, 2):
        sent(send.at[i], send_sem.at[i])
    sent(send_left.at[1], left_send_sem.at[1])
    for half in range(2):
        for u in range(2):
            sent(prod.at[u, half], back_send_sem.at[u, half])
    for copy in outs:
        copy.wait()


def solution(mesh):
    nr, nc = mesh.shape["row"], mesh.shape["col"]

    def local(pair, pad_mask, valid_flags, w_in, w_gate, w_out, gains, shifts):
        H = nr * nc
        C = pair.shape[-1]
        hbm = pl.BlockSpec(memory_space=pl.ANY)
        pad_mask = pad_mask.reshape(-1, 128)
        valid_flags = valid_flags.reshape(-1, 128)
        operands = (pair, pad_mask, valid_flags, w_in, w_gate, w_out, gains, shifts)
        dma = pltpu.SemaphoreType.DMA
        return pl.pallas_call(
            functools.partial(kernel, nr, nc),
            out_shape=jax.ShapeDtypeStruct(pair.shape, BF16),
            in_specs=[hbm] * len(operands),
            out_specs=hbm,
            scratch_shapes=[pltpu.VMEM(a.shape, a.dtype) for a in operands] + [
                pltpu.SMEM(pad_mask.shape, pad_mask.dtype),
                pltpu.SMEM(valid_flags.shape, valid_flags.dtype),
                pltpu.VMEM(pair.shape, BF16),
                pltpu.VMEM((3, H, T, 128), BF16),
                pltpu.VMEM((3, H, T, 128), BF16),
                pltpu.VMEM((2, H, T // 2, 128), BF16),
                pltpu.VMEM((2, H, T // 2, 128), BF16),
                pltpu.VMEM((2, 2, H, T // 2, 128), BF16),
                pltpu.VMEM((2, 2, H, T // 2, 128), BF16),
                pltpu.VMEM((2, 4 * H, C), BF16),
                pltpu.VMEM((2, C, C), BF16),
                pltpu.VMEM((2, C, H), BF16),
                pltpu.VMEM((T // 4, C, 512), BF16),
                pltpu.VMEM((T // 4, C, 512), F32),
                pltpu.VMEM((T, C, 128), BF16),
                pltpu.VMEM((H * T, 128), F32),
                pltpu.VMEM((H * T // 2, 128), F32),
                pltpu.VMEM((nc * 128, nc * 128), BF16),
                pltpu.VMEM((nr * T, nc * 128), BF16),
                dma((10,)), dma((3,)), dma((3,)), dma((2,)), dma((2,)), dma((2, 2)), dma((2, 2)), dma((4,)),
            ],
            compiler_params=pltpu.CompilerParams(
                collective_id=0, has_side_effects=True, vmem_limit_bytes=48 * 1024 * 1024
            ),
        )(*[pltpu.with_memory_space_constraint(a, pltpu.HBM) for a in operands])

    placed = (P("row", "col", None), P(), P(), P(), P(), P(), P(), P())
    return jax.shard_map(
        local, mesh=mesh, in_specs=placed, out_specs=P("row", "col", None), check_vma=False
    )
```

```python
import functools
import itertools

import jax
import jax.numpy as jnp
from jax import lax
from jax.experimental import pallas as pl
from jax.experimental.pallas import tpu as pltpu
from jax.sharding import PartitionSpec as P

EPS = 1e-05
MESH = pl.DeviceIdType.MESH
F32 = jnp.float32
BF16 = jnp.bfloat16
T = 16
HALF = 64
NN = (((1,), (0,)), ((), ()))
NT = (((1,), (1,)), ((), ()))


def sigmoid(v):
    return 0.5 * jnp.tanh(0.5 * v) + 0.5


def dot(a, b, dims=NN):
    return lax.dot_general(a, b, dims, preferred_element_type=F32)


def hops(shift, size):
    return min(shift, size - shift)


def kernel(
    nr, nc, pair_hbm, pad_hbm, valid_hbm, w_in_hbm, w_gate_hbm, w_out_hbm, gain_hbm, shift_hbm,
    out_hbm,
    pair_ref, pad_v, valid_v, w_in_ref, w_gate_ref, w_out_ref, gain_ref, shift_ref, pad_s, valid_s, out_ref,
    send, got, send_left, got_left, prod, back, wt, wg, wo, nb, gate, held, lay, lay2, big, lhs,
    load_sem, send_sem, got_sem, left_send_sem, left_sem, back_send_sem, back_sem, out_sem,
):
    H = nr * nc
    C = pair_ref.shape[-1]
    X, Y = nr // 4, nc // 2
    my_r = lax.axis_index("row")
    my_c = lax.axis_index("col")
    me = my_r * nc + my_c

    xs = [(my_r // 4 + d) % X for d in range(X)]
    ys = [(my_c // 2 + d) % Y for d in range(Y)]
    zs = [((my_c % 2) * 2 + (my_r // 2) % 2 + d) % 4 for d in range(4)]
    ks = [(my_r % 2 + d) % 2 for d in range(2)]
    row_parts = [[xs[dx] * 4 + ks[dk] for dk in range(2)] for dx in range(X)]
    z_lo = [(z % 2) * 2 for z in zs]
    z_hi = [z // 2 for z in zs]

    def peer(shift):
        dx, dy, dz, dk = shift
        return row_parts[dx][dk] + z_lo[dz], ys[dy] * 2 + z_hi[dz]

    def distance(shift):
        dx, dy, dz, dk = shift
        return hops(dx, X) + hops(dy, Y) + hops(dz, 4) + 0.3 * dk

    here = (0, 0, 0, 0)
    shifts = [s for s in itertools.product(range(X), range(Y), range(4), range(2)) if s != here]
    shifts.sort(key=lambda s: (-distance(s), (s[0] * 37 + s[1] * 53 + s[2] * 71 + s[3] * 19) % 29))

    loads = []
    for i, (a, b) in enumerate((
        (pair_hbm, pair_ref), (w_in_hbm, w_in_ref), (gain_hbm, gain_ref), (shift_hbm, shift_ref), (pad_hbm, pad_v),
        (pad_hbm, pad_s), (w_gate_hbm, w_gate_ref), (w_out_hbm, w_out_ref), (valid_hbm, valid_v),
        (valid_hbm, valid_s),
    )):
        copy = pltpu.make_async_copy(a, b, load_sem.at[i])
        copy.start()
        loads.append(copy)

    barrier = pltpu.get_barrier_semaphore()
    for s in shifts:
        pl.semaphore_signal(barrier, inc=1, device_id=peer(s), device_id_type=MESH)

    lane = lax.broadcasted_iota(jnp.int32, (1, 128), 1)
    low = lane < HALF
    odd = my_c % 2

    def col_flags(ref):
        row = ref[pl.ds(my_c // 2, 1), :].astype(F32)
        turned = pltpu.roll(row, HALF, 1)
        lo = jnp.where(odd == 1, turned, row)
        hi = jnp.where(odd == 1, row, turned)
        return jnp.where(low, lo, hi)

    def flag(ref, i):
        return ref[i // 128, i % 128].astype(F32)

    q = 4
    B = T // 2

    def flags(ref, cols, i2):
        tiles = []
        for t in range(q):
            top = flag(ref, my_r * 32 + i2 + t)
            bottom = flag(ref, my_r * 32 + T + i2 + t)
            tiles.append(jnp.where(low, top, bottom) * cols)
        return jnp.concatenate(tiles, axis=1)

    def turn(value):
        return jnp.transpose(value.astype(F32))

    def turn_weights(u):
        turned = turn(w_in_ref[u]).astype(BF16)
        for i, block in enumerate((0, 2, 1, 3)):
            wt[u, i * H:(i + 1) * H] = turned[block * H:(block + 1) * H]

    def turn_small(u):
        wg[u] = turn(w_gate_ref[u]).astype(BF16)
        wo[u] = turn(w_out_ref[u]).astype(BF16)

    def column(ref, u, which, n):
        return jnp.transpose(jnp.broadcast_to(ref[u, which:which + 1, :n], (128, n)))

    def norm(values, gain, shift):
        center = jnp.mean(values, axis=0, keepdims=True)
        centred = values - center
        variance = jnp.mean(centred * centred, axis=0, keepdims=True)
        return (centred * lax.rsqrt(variance + EPS) * gain + shift).astype(BF16)

    def project(u, side, normed, mask, at, stride):
        both = dot(wt[u, side * 2 * H:(side + 1) * 2 * H, :], normed)
        value = both[:H] * (sigmoid(both[H:]) * mask)
        for t in range(q):
            lay[pl.ds(at + t, H, stride=stride), :] = value[:, t * 128:(t + 1) * 128]

    def pack(target, rows):
        hs = min(16, H)

        def some(g, carry):
            part = lay[pl.ds(g * hs * rows, hs * rows), :].astype(BF16)
            target[pl.ds(g * hs, hs)] = part.reshape(hs, rows, 128)
            return carry

        for_each(H // hs, some)

    def for_each(n, step):
        if n:
            lax.fori_loop(0, n, step, 0, unroll=n <= 2)

    def gates(u):
        def chunk(g, carry):
            gate[g] = sigmoid(dot(wg[u], nb[g]))
            return carry

        for_each(T // q, chunk)

    def put(source, target, s_sem, r_sem, some):
        for s in some:
            if s == here:
                pltpu.make_async_copy(source.at[me], target.at[me], r_sem).start()
            else:
                r, c = peer(s)
                pltpu.make_async_remote_copy(
                    src_ref=source.at[r * nc + c], dst_ref=target.at[me], send_sem=s_sem, recv_sem=r_sem,
                    device_id=(r, c), device_id_type=MESH,
                ).start()

    def put_block(i):
        put(send.at[i], got.at[i], send_sem.at[i], got_sem.at[i], shifts + [here])

    def put_left(half):
        put(send_left.at[half], got_left.at[half], left_send_sem.at[half], left_sem.at[half], shifts + [here])

    def put_back(u, half, some):
        put(prod.at[u, half], back.at[u, half], back_send_sem.at[u, half], back_sem.at[u, half], some)

    def arrive(target, r_sem):
        pltpu.make_async_copy(target, target, r_sem).wait()

    def sent(source, s_sem):
        part = source.at[pl.ds(0, H - 1)]
        pltpu.make_async_copy(part, part, s_sem).wait()

    def halves(tile):
        turned = pltpu.roll(tile, HALF, 1)
        zero = jnp.zeros_like(tile)
        return (
            (jnp.where(low, tile, zero).astype(BF16), jnp.where(low, turned, zero).astype(BF16)),
            (jnp.where(low, zero, turned).astype(BF16), jnp.where(low, zero, tile).astype(BF16)),
        )

    def build_outgoing():
        box = got.at[0]

        def step(r, carry):
            for c in range(nc):
                parts = halves(box[r * nc + c].astype(F32))
                for ip in range(2):
                    for p in range(2):
                        at = (r // 2) * 128 + ip * HALF + (r % 2) * 32 + p * T
                        big[pl.ds(pl.multiple_of(at, T), T), c * 128:(c + 1) * 128] = parts[ip][p]
            return carry

        for_each(nr, step)

    def line_up_outgoing(half):
        box = got_left.at[half]
        for c in range(nc):
            for r in range(0, nr, 2):
                pair = jnp.concatenate([box[r * nc + c].astype(F32), box[(r + 1) * nc + c].astype(F32)], axis=0)
                at = half * nr * B + r * B
                lhs[at:at + T, c * 128:(c + 1) * 128] = pair.astype(BF16)

    def build_incoming(half):
        box = got.at[1 + half]

        def step(g, carry):
            r = g * 2
            for c in range(nc):
                tile = jnp.concatenate(
                    [box[r * nc + c].astype(F32)[:B], box[(r + 1) * nc + c].astype(F32)[:B]], axis=0
                )
                parts = halves(tile)
                for ip in range(2):
                    for p in range(2):
                        at = ((ip * 2 + p) * 2 + half) * nr * B + g * T
                        big[pl.ds(pl.multiple_of(at, T), T), c * 128:(c + 1) * 128] = parts[ip][p]
            return carry

        for_each(nr // 2, step)

    def line_up_incoming(half):
        box = got.at[1 + half]
        for c in range(nc):
            block = jnp.concatenate([box[r * nc + c].astype(F32)[B:] for r in range(nr)], axis=0)
            turned = jnp.transpose(block).astype(BF16)
            for kp, hi, ip in itertools.product(range(2), range(2), range(2)):
                src = ((kp * 2 + hi) * 2 + ip) * T
                dst = (c * 2 + hi) * T
                at = ((ip * 2 + kp) * 2 + half) * nr * B
                lhs[dst:dst + T, at:at + nr * B] = turned[src:src + T, :]

    columns = sorted(range(Y), key=lambda d: -hops(d, Y))

    def contract_outgoing(half):
        for dy in columns:
            c0 = ys[dy] * 2
            span = pl.ds(pl.multiple_of(c0 * 128, 256), 256)
            value = dot(lhs[half * nr * B:(half + 1) * nr * B, :], big[span, :], NT)
            for c in range(2):
                part = value[:, c * 128:(c + 1) * 128].astype(BF16).reshape(nr, B, 128)
                for r in range(nr):
                    prod[0, half, r * nc + c0 + c] = part[r]
        put_back(0, half, shifts + [here])

    def contract_incoming():
        for dy in columns:
            c0 = ys[dy] * 2
            span = pl.ds(pl.multiple_of(c0 * 128, 256), 256)
            value = dot(lhs[...], big[:, span])
            for c in range(2):
                part = value[:, c * 128:(c + 1) * 128].astype(BF16).reshape(nr, 2, B, 128)
                for r in range(nr):
                    for half in range(2):
                        prod[1, half, r * nc + c0 + c] = part[r, half]
        put_back(1, 0, shifts + [here])
        put_back(1, 1, shifts + [here])

    def widen(u, half):
        hs = min(16, H)
        box = back.at[u, half]
        arrive(box, back_sem.at[u, half])

        def some(g, carry):
            lay2[pl.ds(g * hs * B, hs * B), :] = box[pl.ds(g * hs, hs)].astype(F32).reshape(hs * B, 128)
            return carry

        for_each(H // hs, some)

    def finish(u, half, row, factors):
        gain, shift = factors
        i2 = half * B + row
        normed = [norm(lay2[pl.ds(row + t, H, stride=B), :], gain, shift) for t in range(q)]
        update = dot(wo[u], jnp.concatenate(normed, axis=1))
        old = jnp.concatenate([held[i2 + t].astype(F32) for t in range(q)], axis=1)
        return old + gate[i2 // q] * update * flags(valid_s, valid_cols, i2)

    def from_pair(i2, n):
        top = pair_ref[pl.ds(i2, n)]
        bottom = pair_ref[pl.ds(i2 + T, n)]
        return jnp.concatenate([top, bottom], axis=1).reshape(n * 128, C)

    for copy in loads[:6]:
        copy.wait()
    turn_weights(0)
    pad_cols = col_flags(pad_v)
    gain, shift = column(gain_ref, 0, 0, C), column(shift_ref, 0, 0, C)

    def right_first(g, carry):
        i2 = g * q
        values = turn(from_pair(i2, q))
        normed = []
        for t in range(q):
            tile = values[:, t * 128:(t + 1) * 128]
            held[i2 + t] = tile.astype(BF16)
            normed.append(norm(tile, gain, shift))
        normed = jnp.concatenate(normed, axis=1)
        nb[g] = normed
        project(0, 1, normed, flags(pad_s, pad_cols, i2), i2, T)
        return carry

    for_each(T // q, right_first)
    pack(send.at[0], T)
    pl.semaphore_wait(barrier, H - 1)
    put_block(0)
    for half in range(2):
        def left_next(g, carry, half=half):
            i2 = half * B + g * q
            project(0, 0, nb[half * (B // q) + g], flags(pad_s, pad_cols, i2), g * q, B)
            return carry

        for_each(B // q, left_next)
        pack(send_left.at[half], B)
        if half == 0:
            for copy in loads[6:]:
                copy.wait()
            turn_small(0)
            gates(0)
            sent(send.at[0], send_sem.at[0])
        else:
            turn_weights(1)
            turn_small(1)
            sent(send_left.at[0], left_send_sem.at[0])
        put_left(half)
    valid_cols = col_flags(valid_v)
    factors = column(gain_ref, 0, 1, H), column(shift_ref, 0, 1, H)
    gain1, shift1 = column(gain_ref, 1, 0, C), column(shift_ref, 1, 0, C)
    arrive(got.at[0], got_sem.at[0])
    build_outgoing()
    for half in range(2):
        arrive(got_left.at[half], left_sem.at[half])
        line_up_outgoing(half)
        contract_outgoing(half)

    for half in range(2):
        widen(0, half)

        def middle(g, carry, half=half):
            i2 = half * B + g * q
            values = finish(0, half, g * q, factors).astype(BF16)
            normed = []
            for t in range(q):
                tile = values[:, t * 128:(t + 1) * 128]
                held[i2 + t] = tile
                normed.append(norm(tile.astype(F32), gain1, shift1))
            normed = jnp.concatenate(normed, axis=1)
            nb[half * (B // q) + g] = normed
            mask = flags(pad_s, pad_cols, i2)
            project(1, 1, normed, mask, g * q, T)
            project(1, 0, normed, mask, B + g * q, T)
            return carry

        for_each(B // q, middle)
        pack(send.at[1 + half], T)
        put_block(1 + half)
    gates(1)
    factors = column(gain_ref, 1, 1, H), column(shift_ref, 1, 1, H)
    for half in range(2):
        arrive(got.at[1 + half], got_sem.at[1 + half])
        build_incoming(half)
        line_up_incoming(half)
    contract_incoming()
    outs = []
    for half in range(2):
        widen(1, half)

        def end(g, carry, half=half):
            values = finish(1, half, g * q, factors)
            for t in range(q):
                i2 = half * B + g * q + t
                value = jnp.transpose(values[:, t * 128:(t + 1) * 128]).astype(BF16)
                out_ref[i2] = value[:HALF]
                out_ref[i2 + T] = value[HALF:]
            return carry

        for_each(B // q, end)
        for i, at in enumerate((half * B, T + half * B)):
            rows = pl.ds(at, B)
            copy = pltpu.make_async_copy(out_ref.at[rows], out_hbm.at[rows], out_sem.at[half * 2 + i])
            copy.start()
            outs.append(copy)
    for i in (1, 2):
        sent(send.at[i], send_sem.at[i])
    sent(send_left.at[1], left_send_sem.at[1])
    for half in range(2):
        for u in range(2):
            sent(prod.at[u, half], back_send_sem.at[u, half])
    for copy in outs:
        copy.wait()


def solution(mesh):
    nr, nc = mesh.shape["row"], mesh.shape["col"]

    def local(pair, pad_mask, valid_flags, w_in, w_gate, w_out, gains, shifts):
        H = nr * nc
        C = pair.shape[-1]
        hbm = pl.BlockSpec(memory_space=pl.ANY)
        pad_mask = pad_mask.reshape(-1, 128)
        valid_flags = valid_flags.reshape(-1, 128)
        operands = (pair, pad_mask, valid_flags, w_in, w_gate, w_out, gains, shifts)
        dma = pltpu.SemaphoreType.DMA
        return pl.pallas_call(
            functools.partial(kernel, nr, nc),
            out_shape=jax.ShapeDtypeStruct(pair.shape, BF16),
            in_specs=[hbm] * len(operands),
            out_specs=hbm,
            scratch_shapes=[pltpu.VMEM(a.shape, a.dtype) for a in operands] + [
                pltpu.SMEM(pad_mask.shape, pad_mask.dtype),
                pltpu.SMEM(valid_flags.shape, valid_flags.dtype),
                pltpu.VMEM(pair.shape, BF16),
                pltpu.VMEM((3, H, T, 128), BF16),
                pltpu.VMEM((3, H, T, 128), BF16),
                pltpu.VMEM((2, H, T // 2, 128), BF16),
                pltpu.VMEM((2, H, T // 2, 128), BF16),
                pltpu.VMEM((2, 2, H, T // 2, 128), BF16),
                pltpu.VMEM((2, 2, H, T // 2, 128), BF16),
                pltpu.VMEM((2, 4 * H, C), BF16),
                pltpu.VMEM((2, C, C), BF16),
                pltpu.VMEM((2, C, H), BF16),
                pltpu.VMEM((T // 4, C, 512), BF16),
                pltpu.VMEM((T // 4, C, 512), F32),
                pltpu.VMEM((T, C, 128), BF16),
                pltpu.VMEM((H * T, 128), F32),
                pltpu.VMEM((H * T // 2, 128), F32),
                pltpu.VMEM((nc * 128, nc * 128), BF16),
                pltpu.VMEM((nr * T, nc * 128), BF16),
                dma((10,)), dma((3,)), dma((3,)), dma((2,)), dma((2,)), dma((2, 2)), dma((2, 2)), dma((4,)),
            ],
            compiler_params=pltpu.CompilerParams(
                collective_id=0, has_side_effects=True, vmem_limit_bytes=48 * 1024 * 1024
            ),
        )(*[pltpu.with_memory_space_constraint(a, pltpu.HBM) for a in operands])

    placed = (P("row", "col", None), P(), P(), P(), P(), P(), P(), P())
    return jax.shard_map(
        local, mesh=mesh, in_specs=placed, out_specs=P("row", "col", None), check_vma=False
    )
```

```python
import functools
import itertools

import jax
import jax.numpy as jnp
from jax import lax
from jax.experimental import pallas as pl
from jax.experimental.pallas import tpu as pltpu
from jax.sharding import PartitionSpec as P

EPS = 1e-05
MESH = pl.DeviceIdType.MESH
F32 = jnp.float32
BF16 = jnp.bfloat16
T = 16
HALF = 64
NN = (((1,), (0,)), ((), ()))
NT = (((1,), (1,)), ((), ()))


def sigmoid(v):
    return 0.5 * jnp.tanh(0.5 * v) + 0.5


def dot(a, b, dims=NN):
    return lax.dot_general(a, b, dims, preferred_element_type=F32)


def hops(shift, size):
    return min(shift, size - shift)


def kernel(
    nr, nc, pair_hbm, pad_hbm, valid_hbm, w_in_hbm, w_gate_hbm, w_out_hbm, gain_hbm, shift_hbm,
    out_hbm,
    pair_ref, pad_v, valid_v, w_in_ref, w_gate_ref, w_out_ref, gain_ref, shift_ref, pad_s, valid_s, out_ref,
    send, got, send_left, got_left, prod, back, wt, wg, wo, nb, gate, held, lay, lay2, big, lhs,
    load_sem, send_sem, got_sem, left_send_sem, left_sem, back_send_sem, back_sem, out_sem,
):
    H = nr * nc
    C = pair_ref.shape[-1]
    X, Y = nr // 4, nc // 2
    my_r = lax.axis_index("row")
    my_c = lax.axis_index("col")
    me = my_r * nc + my_c

    xs = [(my_r // 4 + d) % X for d in range(X)]
    ys = [(my_c // 2 + d) % Y for d in range(Y)]
    zs = [((my_c % 2) * 2 + (my_r // 2) % 2 + d) % 4 for d in range(4)]
    ks = [(my_r % 2 + d) % 2 for d in range(2)]
    row_parts = [[xs[dx] * 4 + ks[dk] for dk in range(2)] for dx in range(X)]
    z_lo = [(z % 2) * 2 for z in zs]
    z_hi = [z // 2 for z in zs]

    def peer(shift):
        dx, dy, dz, dk = shift
        return row_parts[dx][dk] + z_lo[dz], ys[dy] * 2 + z_hi[dz]

    def distance(shift):
        dx, dy, dz, dk = shift
        return hops(dx, X) + hops(dy, Y) + hops(dz, 4) + 0.3 * dk

    here = (0, 0, 0, 0)
    shifts = [s for s in itertools.product(range(X), range(Y), range(4), range(2)) if s != here]
    shifts.sort(key=lambda s: (-distance(s), (s[0] * 37 + s[1] * 53 + s[2] * 71 + s[3] * 19) % 29))

    loads = []
    for i, (a, b) in enumerate((
        (pair_hbm, pair_ref), (w_in_hbm, w_in_ref), (gain_hbm, gain_ref), (shift_hbm, shift_ref), (pad_hbm, pad_v),
        (pad_hbm, pad_s), (w_gate_hbm, w_gate_ref), (w_out_hbm, w_out_ref), (valid_hbm, valid_v),
        (valid_hbm, valid_s),
    )):
        copy = pltpu.make_async_copy(a, b, load_sem.at[i])
        copy.start()
        loads.append(copy)

    barrier = pltpu.get_barrier_semaphore()
    for s in shifts:
        pl.semaphore_signal(barrier, inc=1, device_id=peer(s), device_id_type=MESH)

    lane = lax.broadcasted_iota(jnp.int32, (1, 128), 1)
    low = lane < HALF
    odd = my_c % 2

    def col_flags(ref):
        row = ref[pl.ds(my_c // 2, 1), :].astype(F32)
        turned = pltpu.roll(row, HALF, 1)
        lo = jnp.where(odd == 1, turned, row)
        hi = jnp.where(odd == 1, row, turned)
        return jnp.where(low, lo, hi)

    def flag(ref, i):
        return ref[i // 128, i % 128].astype(F32)

    q = 4
    B = T // 2

    def flags(ref, cols, i2):
        tiles = []
        for t in range(q):
            top = flag(ref, my_r * 32 + i2 + t)
            bottom = flag(ref, my_r * 32 + T + i2 + t)
            tiles.append(jnp.where(low, top, bottom) * cols)
        return jnp.concatenate(tiles, axis=1)

    def turn(value):
        return jnp.transpose(value.astype(F32))

    def turn_weights(u):
        turned = turn(w_in_ref[u]).astype(BF16)
        for i, block in enumerate((0, 2, 1, 3)):
            wt[u, i * H:(i + 1) * H] = turned[block * H:(block + 1) * H]

    def turn_small(u):
        wg[u] = turn(w_gate_ref[u]).astype(BF16)
        wo[u] = turn(w_out_ref[u]).astype(BF16)

    def column(ref, u, which, n):
        return jnp.transpose(jnp.broadcast_to(ref[u, which:which + 1, :n], (128, n)))

    def norm(values, gain, shift):
        center = jnp.mean(values, axis=0, keepdims=True)
        centred = values - center
        variance = jnp.mean(centred * centred, axis=0, keepdims=True)
        return (centred * lax.rsqrt(variance + EPS) * gain + shift).astype(BF16)

    def project(u, side, normed, mask, at, stride):
        place(dot(wt[u, side * 2 * H:(side + 1) * 2 * H, :], normed), mask, at, stride)

    def place(both, mask, at, stride):
        value = both[:H] * (sigmoid(both[H:]) * mask)
        for t in range(q):
            lay[pl.ds(at + t, H, stride=stride), :] = value[:, t * 128:(t + 1) * 128]

    def pack(target, rows):
        hs = min(16, H)

        def some(g, carry):
            part = lay[pl.ds(g * hs * rows, hs * rows), :].astype(BF16)
            target[pl.ds(g * hs, hs)] = part.reshape(hs, rows, 128)
            return carry

        for_each(H // hs, some)

    def for_each(n, step):
        if n:
            lax.fori_loop(0, n, step, 0, unroll=n <= 2)

    def gates(u):
        def chunk(g, carry):
            gate[g] = sigmoid(dot(wg[u], nb[g]))
            return carry

        for_each(T // q, chunk)

    def put(source, target, s_sem, r_sem, some):
        for s in some:
            if s == here:
                pltpu.make_async_copy(source.at[me], target.at[me], r_sem).start()
            else:
                r, c = peer(s)
                pltpu.make_async_remote_copy(
                    src_ref=source.at[r * nc + c], dst_ref=target.at[me], send_sem=s_sem, recv_sem=r_sem,
                    device_id=(r, c), device_id_type=MESH,
                ).start()

    def put_block(i):
        put(send.at[i], got.at[i], send_sem.at[i], got_sem.at[i], shifts + [here])

    def put_left(half):
        put(send_left.at[half], got_left.at[half], left_send_sem.at[half], left_sem.at[half], shifts + [here])

    def put_back(u, half, some):
        put(prod.at[u, half], back.at[u, half], back_send_sem.at[u, half], back_sem.at[u, half], some)

    def arrive(target, r_sem):
        pltpu.make_async_copy(target, target, r_sem).wait()

    def sent(source, s_sem):
        part = source.at[pl.ds(0, H - 1)]
        pltpu.make_async_copy(part, part, s_sem).wait()

    def halves(tile):
        turned = pltpu.roll(tile, HALF, 1)
        zero = jnp.zeros_like(tile)
        return (
            (jnp.where(low, tile, zero).astype(BF16), jnp.where(low, turned, zero).astype(BF16)),
            (jnp.where(low, zero, turned).astype(BF16), jnp.where(low, zero, tile).astype(BF16)),
        )

    def build_outgoing():
        box = got.at[0]

        def step(r, carry):
            for c in range(nc):
                parts = halves(box[r * nc + c].astype(F32))
                for ip in range(2):
                    for p in range(2):
                        at = (r // 2) * 128 + ip * HALF + (r % 2) * 32 + p * T
                        big[pl.ds(pl.multiple_of(at, T), T), c * 128:(c + 1) * 128] = parts[ip][p]
            return carry

        for_each(nr, step)

    def line_up_outgoing(half):
        box = got_left.at[half]
        for c in range(nc):
            for r in range(0, nr, 2):
                pair = jnp.concatenate([box[r * nc + c].astype(F32), box[(r + 1) * nc + c].astype(F32)], axis=0)
                at = half * nr * B + r * B
                lhs[at:at + T, c * 128:(c + 1) * 128] = pair.astype(BF16)

    def build_incoming(half):
        box = got.at[1 + half]

        def step(g, carry):
            r = g * 2
            for c in range(nc):
                tile = jnp.concatenate(
                    [box[r * nc + c].astype(F32)[:B], box[(r + 1) * nc + c].astype(F32)[:B]], axis=0
                )
                parts = halves(tile)
                for ip in range(2):
                    for p in range(2):
                        at = ((ip * 2 + p) * 2 + half) * nr * B + g * T
                        big[pl.ds(pl.multiple_of(at, T), T), c * 128:(c + 1) * 128] = parts[ip][p]
            return carry

        for_each(nr // 2, step)

    def line_up_incoming(half):
        box = got.at[1 + half]
        for c in range(nc):
            block = jnp.concatenate([box[r * nc + c].astype(F32)[B:] for r in range(nr)], axis=0)
            turned = jnp.transpose(block).astype(BF16)
            for kp, hi, ip in itertools.product(range(2), range(2), range(2)):
                src = ((kp * 2 + hi) * 2 + ip) * T
                dst = (c * 2 + hi) * T
                at = ((ip * 2 + kp) * 2 + half) * nr * B
                lhs[dst:dst + T, at:at + nr * B] = turned[src:src + T, :]

    columns = sorted(range(Y), key=lambda d: -hops(d, Y))

    def contract_outgoing(half):
        for dy in columns:
            c0 = ys[dy] * 2
            span = pl.ds(pl.multiple_of(c0 * 128, 256), 256)
            value = dot(lhs[half * nr * B:(half + 1) * nr * B, :], big[span, :], NT)
            for c in range(2):
                part = value[:, c * 128:(c + 1) * 128].astype(BF16).reshape(nr, B, 128)
                for r in range(nr):
                    prod[0, half, r * nc + c0 + c] = part[r]
        put_back(0, half, shifts + [here])

    def contract_incoming():
        for dy in columns:
            c0 = ys[dy] * 2
            span = pl.ds(pl.multiple_of(c0 * 128, 256), 256)
            value = dot(lhs[...], big[:, span])
            for c in range(2):
                part = value[:, c * 128:(c + 1) * 128].astype(BF16).reshape(nr, 2, B, 128)
                for r in range(nr):
                    for half in range(2):
                        prod[1, half, r * nc + c0 + c] = part[r, half]
        put_back(1, 0, shifts + [here])
        put_back(1, 1, shifts + [here])

    def widen(u, half):
        hs = min(16, H)
        box = back.at[u, half]
        arrive(box, back_sem.at[u, half])

        def some(g, carry):
            lay2[pl.ds(g * hs * B, hs * B), :] = box[pl.ds(g * hs, hs)].astype(F32).reshape(hs * B, 128)
            return carry

        for_each(H // hs, some)

    def finish(u, half, row, factors):
        gain, shift = factors
        i2 = half * B + row
        normed = [norm(lay2[pl.ds(row + t, H, stride=B), :], gain, shift) for t in range(q)]
        update = dot(wo[u], jnp.concatenate(normed, axis=1))
        old = jnp.concatenate([held[i2 + t].astype(F32) for t in range(q)], axis=1)
        return old + gate[i2 // q] * update * flags(valid_s, valid_cols, i2)

    def from_pair(i2, n):
        top = pair_ref[pl.ds(i2, n)]
        bottom = pair_ref[pl.ds(i2 + T, n)]
        return jnp.concatenate([top, bottom], axis=1).reshape(n * 128, C)

    for copy in loads[:6]:
        copy.wait()
    turn_weights(0)
    pad_cols = col_flags(pad_v)
    gain, shift = column(gain_ref, 0, 0, C), column(shift_ref, 0, 0, C)

    def right_first(g, carry):
        i2 = g * q
        values = turn(from_pair(i2, q))
        normed = []
        for t in range(q):
            tile = values[:, t * 128:(t + 1) * 128]
            held[i2 + t] = tile.astype(BF16)
            normed.append(norm(tile, gain, shift))
        normed = jnp.concatenate(normed, axis=1)
        nb[g] = normed
        project(0, 1, normed, flags(pad_s, pad_cols, i2), i2, T)
        return carry

    for_each(T // q, right_first)
    pack(send.at[0], T)
    pl.semaphore_wait(barrier, H - 1)
    put_block(0)
    for half in range(2):
        def left_next(g, carry, half=half):
            i2 = half * B + g * q
            project(0, 0, nb[half * (B // q) + g], flags(pad_s, pad_cols, i2), g * q, B)
            return carry

        for_each(B // q, left_next)
        pack(send_left.at[half], B)
        if half == 0:
            for copy in loads[6:]:
                copy.wait()
            turn_small(0)
            gates(0)
            sent(send.at[0], send_sem.at[0])
        else:
            turn_weights(1)
            turn_small(1)
            sent(send_left.at[0], left_send_sem.at[0])
        put_left(half)
    valid_cols = col_flags(valid_v)
    factors = column(gain_ref, 0, 1, H), column(shift_ref, 0, 1, H)
    gain1, shift1 = column(gain_ref, 1, 0, C), column(shift_ref, 1, 0, C)
    arrive(got.at[0], got_sem.at[0])
    build_outgoing()
    for half in range(2):
        arrive(got_left.at[half], left_sem.at[half])
        line_up_outgoing(half)
        contract_outgoing(half)

    for half in range(2):
        widen(0, half)

        def middle(g, carry, half=half):
            i2 = half * B + g * q
            values = finish(0, half, g * q, factors).astype(BF16)
            normed = []
            for t in range(q):
                tile = values[:, t * 128:(t + 1) * 128]
                held[i2 + t] = tile
                normed.append(norm(tile.astype(F32), gain1, shift1))
            normed = jnp.concatenate(normed, axis=1)
            nb[half * (B // q) + g] = normed
            mask = flags(pad_s, pad_cols, i2)
            every = dot(wt[1], normed)
            place(every[2 * H:], mask, g * q, T)
            place(every[:2 * H], mask, B + g * q, T)
            return carry

        for_each(B // q, middle)
        pack(send.at[1 + half], T)
        put_block(1 + half)
    gates(1)
    factors = column(gain_ref, 1, 1, H), column(shift_ref, 1, 1, H)
    for half in range(2):
        arrive(got.at[1 + half], got_sem.at[1 + half])
        build_incoming(half)
        line_up_incoming(half)
    contract_incoming()
    outs = []
    for half in range(2):
        widen(1, half)

        def end(g, carry, half=half):
            values = finish(1, half, g * q, factors)
            for t in range(q):
                i2 = half * B + g * q + t
                value = jnp.transpose(values[:, t * 128:(t + 1) * 128]).astype(BF16)
                out_ref[i2] = value[:HALF]
                out_ref[i2 + T] = value[HALF:]
            return carry

        for_each(B // q, end)
        for i, at in enumerate((half * B, T + half * B)):
            rows = pl.ds(at, B)
            copy = pltpu.make_async_copy(out_ref.at[rows], out_hbm.at[rows], out_sem.at[half * 2 + i])
            copy.start()
            outs.append(copy)
    for i in (1, 2):
        sent(send.at[i], send_sem.at[i])
    sent(send_left.at[1], left_send_sem.at[1])
    for half in range(2):
        for u in range(2):
            sent(prod.at[u, half], back_send_sem.at[u, half])
    for copy in outs:
        copy.wait()


def solution(mesh):
    nr, nc = mesh.shape["row"], mesh.shape["col"]

    def local(pair, pad_mask, valid_flags, w_in, w_gate, w_out, gains, shifts):
        H = nr * nc
        C = pair.shape[-1]
        hbm = pl.BlockSpec(memory_space=pl.ANY)
        pad_mask = pad_mask.reshape(-1, 128)
        valid_flags = valid_flags.reshape(-1, 128)
        operands = (pair, pad_mask, valid_flags, w_in, w_gate, w_out, gains, shifts)
        dma = pltpu.SemaphoreType.DMA
        return pl.pallas_call(
            functools.partial(kernel, nr, nc),
            out_shape=jax.ShapeDtypeStruct(pair.shape, BF16),
            in_specs=[hbm] * len(operands),
            out_specs=hbm,
            scratch_shapes=[pltpu.VMEM(a.shape, a.dtype) for a in operands] + [
                pltpu.SMEM(pad_mask.shape, pad_mask.dtype),
                pltpu.SMEM(valid_flags.shape, valid_flags.dtype),
                pltpu.VMEM(pair.shape, BF16),
                pltpu.VMEM((3, H, T, 128), BF16),
                pltpu.VMEM((3, H, T, 128), BF16),
                pltpu.VMEM((2, H, T // 2, 128), BF16),
                pltpu.VMEM((2, H, T // 2, 128), BF16),
                pltpu.VMEM((2, 2, H, T // 2, 128), BF16),
                pltpu.VMEM((2, 2, H, T // 2, 128), BF16),
                pltpu.VMEM((2, 4 * H, C), BF16),
                pltpu.VMEM((2, C, C), BF16),
                pltpu.VMEM((2, C, H), BF16),
                pltpu.VMEM((T // 4, C, 512), BF16),
                pltpu.VMEM((T // 4, C, 512), F32),
                pltpu.VMEM((T, C, 128), BF16),
                pltpu.VMEM((H * T, 128), F32),
                pltpu.VMEM((H * T // 2, 128), F32),
                pltpu.VMEM((nc * 128, nc * 128), BF16),
                pltpu.VMEM((nr * T, nc * 128), BF16),
                dma((10,)), dma((3,)), dma((3,)), dma((2,)), dma((2,)), dma((2, 2)), dma((2, 2)), dma((4,)),
            ],
            compiler_params=pltpu.CompilerParams(
                collective_id=0, has_side_effects=True, vmem_limit_bytes=48 * 1024 * 1024
            ),
        )(*[pltpu.with_memory_space_constraint(a, pltpu.HBM) for a in operands])

    placed = (P("row", "col", None), P(), P(), P(), P(), P(), P(), P())
    return jax.shard_map(
        local, mesh=mesh, in_specs=placed, out_specs=P("row", "col", None), check_vma=False
    )
```
